128 devices in a mesh: row: 8 (over z, y_hi), col: 16 (over y_lo, x, core).
Axes of the slice: x: 4, y: 4 (y_hi: 2, y_lo: 2; y = y_hi * 2 + y_lo), z: 4, core: 2. Of those that a mesh axis runs over, the one named last changes fastest.
Arguments:
- coarse_latent: bfloat16 [320, 128, 256], P(None, ('row', 'col')), may hold values from -6 to 6
- fine_latent: bfloat16 [512, 327680], P('row', 'col'), may hold values from -6 to 6
- timestep: int32 [1], replicated, may hold values from 12 to 19
- coarse_first: bfloat16 [3, 3, 320, 320], replicated, may hold values from -0.1875 to 0.1875
- coarse_second: bfloat16 [3, 3, 320, 320], replicated, may hold values from -0.1875 to 0.1875
- local_weight: bfloat16 [3, 3, 320, 320], replicated, may hold values from -0.1875 to 0.1875
- dilated_weight: bfloat16 [3, 3, 320, 320], replicated, may hold values from -0.1875 to 0.1875
Outputs:
- blended: float32 [512, 327680], P('row', 'col')
The draws below stay inside these ranges and needn't reach their ends.
All inputs are finite; a program needn't handle non-finite values.
Results may differ from the reference program's by a relative error of at most 0.0025.
Values may be sent and summed in bfloat16 or wider, within the bound.
A program may use at most 320 MiB of HBM per device.

```python
import math
import jax
import jax.numpy as jnp

C = 320
SCALE = 4
STEPS = 50
HC = 128
WC = 256
HF = 512
WF = 1024


def level_of(rng, extent, cuts, least, top_value):
    def one(dim, shards_of):
        steps = jax.random.uniform(jax.random.fold_in(jax.random.fold_in(rng, 6), dim), (shards_of,), jnp.float32, least / len(cuts), top_value / len(cuts))
        return jnp.repeat(jnp.exp(steps), extent[dim] // shards_of).reshape((-1,) + (1,) * (len(extent) - dim - 1))

    gain = one(*cuts[0])
    for cut in cuts[1:]:
        gain = gain * one(*cut)
    return gain


def normal_values(rng, shape, width, limit, shards=(), kind=jnp.bfloat16):
    array = jax.random.normal(rng, shape, jnp.float32) * width
    if len(shards) > 0:
        array = level_of(rng, shape, shards, -0.22, 0.18) * array
    return jnp.clip(array, min=-limit, max=limit).astype(kind)


def setup_inputs(seed: int = 0) -> dict:
    key_list = jax.random.split(jax.random.key(seed), 8)
    return {
        "coarse_latent": normal_values(key_list[0], (C, HC, WC), 1.0, 6.0, ((1, 128),)),
        "fine_latent": normal_values(key_list[1], (HF, WF * C), 1.0, 6.0, ((0, 8), (1, 16))),
        "timestep": jax.random.randint(key_list[2], (1,), 12, 20).astype(jnp.int32),
        "coarse_first": normal_values(key_list[3], (3, 3, C, C), (3 * C) ** -0.5, 0.1875),
        "coarse_second": normal_values(key_list[4], (3, 3, C, C), (3 * C) ** -0.5, 0.1875),
        "local_weight": normal_values(key_list[5], (3, 3, C, C), (3 * C) ** -0.5, 0.1875),
        "dilated_weight": normal_values(key_list[6], (3, 3, C, C), (3 * C) ** -0.5, 0.1875),
    }


def silu_round(values):
    return jax.nn.silu(values.astype(jnp.float32)).astype(jnp.bfloat16)


def convolve(padded, weight, dilation, offset, height, breadth):
    summed = jnp.zeros((weight.shape[2], height, breadth), jnp.float32)
    for tap_row in range(3):
        for tap_col in range(3):
            top = offset + tap_row * dilation
            left = offset + tap_col * dilation
            window = padded[:, top:top + height, left:left + breadth].astype(jnp.float32)
            summed = summed + jnp.einsum("oc,chw->ohw", weight[tap_row, tap_col].astype(jnp.float32), window)
    return summed


def upsample(padded, factor):
    inner_rows = padded.shape[1] - 2
    inner_cols = padded.shape[2] - 2
    phases = []
    for phase in range(factor):
        offset = (phase + 0.5) / factor - 0.5
        if offset < 0:
            phases.append(-offset * padded[:, 0:inner_rows] + (1.0 + offset) * padded[:, 1:inner_rows + 1])
        else:
            phases.append((1.0 - offset) * padded[:, 1:inner_rows + 1] + offset * padded[:, 2:inner_rows + 2])
    rowwise = jnp.stack(phases, axis=2).reshape(padded.shape[0], inner_rows * factor, padded.shape[2])
    phases = []
    for phase in range(factor):
        offset = (phase + 0.5) / factor - 0.5
        if offset < 0:
            phases.append(-offset * rowwise[:, :, 0:inner_cols] + (1.0 + offset) * rowwise[:, :, 1:inner_cols + 1])
        else:
            phases.append((1.0 - offset) * rowwise[:, :, 1:inner_cols + 1] + offset * rowwise[:, :, 2:inner_cols + 2])
    return jnp.stack(phases, axis=3).reshape(padded.shape[0], inner_rows * factor, inner_cols * factor)


def reference(coarse_latent, fine_latent, timestep, coarse_first, coarse_second, local_weight, dilated_weight):
    weight_now = (1.0 + jnp.cos(math.pi * timestep[0].astype(jnp.float32) / STEPS)) / 2.0
    skip = weight_now ** 3
    first_act = silu_round(coarse_latent)
    hidden = convolve(jnp.pad(first_act, ((0, 0), (1, 1), (1, 1))), coarse_first, 1, 0, HC, WC)
    second_act = silu_round(hidden)
    coarse_out = coarse_latent.astype(jnp.float32) + convolve(jnp.pad(second_act, ((0, 0), (1, 1), (1, 1))), coarse_second, 1, 0, HC, WC)
    upsampled = upsample(jnp.pad(coarse_out, ((0, 0), (1, 1), (1, 1)), mode="edge"), SCALE)
    fine_field = jnp.transpose(fine_latent.reshape(HF, WF, C), (2, 0, 1))
    fine_act = jnp.pad(silu_round(fine_field), ((0, 0), (SCALE, SCALE), (SCALE, SCALE)))
    local_out = convolve(fine_act, local_weight, 1, SCALE - 1, HF, WF)
    dilated_out = convolve(fine_act, dilated_weight, SCALE, 0, HF, WF)
    denoised = fine_field.astype(jnp.float32) + weight_now * dilated_out + (1.0 - weight_now) * local_out
    result = skip * upsampled + (1.0 - skip) * denoised
    return jnp.transpose(result, (1, 2, 0)).reshape(HF, WF * C)
```

```python
import functools
import math

import jax
import jax.numpy as jnp
from jax import lax
from jax.experimental import pallas as pl
from jax.experimental.pallas import tpu as pltpu
from jax.sharding import PartitionSpec as P

STEPS = 50
C = 320
ROWS = 8
COLS = 16
PAIR = 2 * C
TALL = 64
PAIRS = 32
CHUNK = 8
CELLS = CHUNK * TALL
SHIFTS = (-4, -1, 0, 1, 4)
KEYS = 6144
PITCH = 20
MESH = pl.DeviceIdType.MESH
VMEM_LIMIT = 60 * 1024 * 1024


def silu(x):
    return x / (1.0 + jnp.exp(-x))


def exchange_kernel(
    fine, coarse, left, right, top, bottom, top_left, top_right, bottom_left, bottom_right, patch,
    rows_in, packed, zero_side, zero_flat, zero_patch, local_sem, send_sem, recv_sem, patch_send, patch_recv,
):
    r = lax.axis_index("row")
    c = lax.axis_index("col")

    def at(dr, dc):
        return (r + dr, c + dc)

    def present(dr, dc):
        ok = None
        for cond, need in ((r > 0, dr < 0), (r < ROWS - 1, dr > 0), (c > 0, dc < 0), (c < COLS - 1, dc > 0)):
            if need:
                ok = cond if ok is None else jnp.logical_and(ok, cond)
        return ok

    barrier = pltpu.get_barrier_semaphore()

    def greet(dev):
        pl.semaphore_signal(barrier, inc=1, device_id=dev, device_id_type=MESH)

    above = r > 0
    below = r < ROWS - 1

    def greet_row(step, _):
        other = lax.rem(c + step, COLS)
        greet((r, other))
        return 0

    lax.fori_loop(1, COLS, greet_row, 0)
    ndiag = ((-1, -1), (-1, 0), (-1, 1), (1, -1), (1, 0), (1, 1))

    def greet_all(dr, cond):
        @pl.when(cond)
        def _():
            def one(step, _):
                greet((r + dr, step))
                return 0
            lax.fori_loop(0, COLS, one, 0)

    greet_all(-1, above)
    greet_all(1, below)
    expected = COLS - 1 + jnp.where(above, COLS, 0) + jnp.where(below, COLS, 0)
    load_top = pltpu.make_async_copy(fine.at[pl.ds(0, 16), :], rows_in.at[0], local_sem.at[0])
    load_low = pltpu.make_async_copy(fine.at[pl.ds(48, 16), :], rows_in.at[1], local_sem.at[1])
    load_top.start()
    load_low.start()
    zero_side[...] = jnp.zeros_like(zero_side)
    zero_flat[...] = jnp.zeros_like(zero_flat)
    zero_patch[...] = jnp.zeros_like(zero_patch)
    load_top.wait()
    load_low.wait()
    for slot, first in ((0, 0), (1, 12)):
        for g in range(4):
            block = rows_in[slot, :, 5120 * g : 5120 * (g + 1)].astype(jnp.float32)
            packed[slot, 4 * g : 4 * g + 4, :] = block[first : first + 4]
    pieces = packed[...].astype(jnp.bfloat16)
    rows_in[0, :, 0:5120] = pieces[0]
    rows_in[1, :, 0:5120] = pieces[1]
    pl.semaphore_wait(barrier, expected)

    sides = (
        ((0, 1), fine.at[:, pl.ds(20480 - 1280, 1280)], left, 0, zero_side),
        ((0, -1), fine.at[:, pl.ds(0, 1280)], right, 1, zero_side),
        ((1, 0), rows_in.at[1, :, pl.ds(0, 5120)], top, 2, zero_flat),
        ((-1, 0), rows_in.at[0, :, pl.ds(0, 5120)], bottom, 3, zero_flat),
        ((1, 1), fine.at[pl.ds(48, 16), pl.ds(20480 - 1280, 1280)], top_left, 4, zero_side.at[pl.ds(0, 16), :]),
        ((1, -1), fine.at[pl.ds(48, 16), pl.ds(0, 1280)], top_right, 5, zero_side.at[pl.ds(0, 16), :]),
        ((-1, 1), fine.at[pl.ds(0, 16), pl.ds(20480 - 1280, 1280)], bottom_left, 6, zero_side.at[pl.ds(0, 16), :]),
        ((-1, -1), fine.at[pl.ds(0, 16), pl.ds(0, 1280)], bottom_right, 7, zero_side.at[pl.ds(0, 16), :]),
    )

    def side_copy(step, src, dst, k):
        return pltpu.make_async_remote_copy(
            src_ref=src, dst_ref=dst, send_sem=send_sem.at[k], recv_sem=recv_sem.at[k],
            device_id=at(*step), device_id_type=MESH)

    for step, src, dst, k, zero in sides:
        @pl.when(present(*step))
        def _(step=step, src=src, dst=dst, k=k):
            side_copy(step, src, dst, k).start()

        @pl.when(jnp.logical_not(present(-step[0], -step[1])))
        def _(dst=dst, k=k, zero=zero):
            pltpu.make_async_copy(zero, dst, recv_sem.at[k]).start()

    def window(target):
        return coarse.at[pl.ds(pl.multiple_of(16 * target, 16), 32), :]

    def patch_copy(dev_r, dev_c, k, slot):
        return pltpu.make_async_remote_copy(
            src_ref=window(dev_c), dst_ref=patch.at[k], send_sem=patch_send.at[slot, dev_c],
            recv_sem=patch_recv.at[k], device_id=(dev_r, dev_c), device_id_type=MESH)

    own = pltpu.make_async_copy(window(c), patch.at[c + 3], patch_recv.at[c + 3])
    own.start()

    def send_row(step, _):
        patch_copy(r, lax.rem(c + step, COLS), c + 3, 0).start()
        return 0

    lax.fori_loop(1, COLS, send_row, 0)
    down = jnp.logical_and(below, c >= 13)
    up = jnp.logical_and(above, c < 3)

    @pl.when(down)
    def _():
        def one(step, _):
            patch_copy(r + 1, lax.rem(c + step, COLS), c - 13, 1).start()
            return 0
        lax.fori_loop(0, COLS, one, 0)

    @pl.when(up)
    def _():
        def one(step, _):
            patch_copy(r - 1, lax.rem(c + step, COLS), c + 19, 1).start()
            return 0
        lax.fori_loop(0, COLS, one, 0)

    for k in (0, 1, 2):
        @pl.when(jnp.logical_not(above))
        def _(k=k):
            pltpu.make_async_copy(zero_patch, patch.at[k], patch_recv.at[k]).start()
    for k in (19, 20, 21):
        @pl.when(jnp.logical_not(below))
        def _(k=k):
            pltpu.make_async_copy(zero_patch, patch.at[k], patch_recv.at[k]).start()

    for step, src, dst, k, zero in sides:
        pltpu.make_async_copy(zero, dst, recv_sem.at[k]).wait()

    def got(k, _):
        pltpu.make_async_copy(zero_patch, patch.at[k], patch_recv.at[k]).wait()
        return 0

    lax.fori_loop(0, 22, got, 0)
    for step, src, dst, k, zero in sides:
        @pl.when(present(*step))
        def _(step=step, src=src, dst=dst, k=k):
            side_copy(step, src, dst, k).wait_send()

    def sent_row(step, _):
        patch_copy(r, lax.rem(c + step, COLS), c + 3, 0).wait_send()
        return 0

    lax.fori_loop(1, COLS, sent_row, 0)

    @pl.when(down)
    def _():
        def one(step, _):
            patch_copy(r + 1, lax.rem(c + step, COLS), c - 13, 1).wait_send()
            return 0
        lax.fori_loop(0, COLS, one, 0)

    @pl.when(up)
    def _():
        def one(step, _):
            patch_copy(r - 1, lax.rem(c + step, COLS), c + 19, 1).wait_send()
            return 0
        lax.fori_loop(0, COLS, one, 0)


def exchange(fine, coarse):
    bf = jnp.bfloat16
    side = jax.ShapeDtypeStruct((64, 1280), bf)
    flat = jax.ShapeDtypeStruct((16, 5120), bf)
    corner = jax.ShapeDtypeStruct((16, 1280), bf)
    return pl.pallas_call(
        exchange_kernel,
        out_shape=(side, side, flat, flat, corner, corner, corner, corner, jax.ShapeDtypeStruct((22, 32, 384), bf)),
        in_specs=[pl.BlockSpec(memory_space=pl.ANY)] * 2,
        out_specs=[pl.BlockSpec(memory_space=pl.ANY)] * 9,
        scratch_shapes=[
            pltpu.VMEM((2, 16, 20480), bf),
            pltpu.VMEM((2, 16, 5120), jnp.float32),
            pltpu.VMEM((64, 1280), bf),
            pltpu.VMEM((16, 5120), bf),
            pltpu.VMEM((32, 384), bf),
            pltpu.SemaphoreType.DMA((2,)),
            pltpu.SemaphoreType.DMA((8,)),
            pltpu.SemaphoreType.DMA((8,)),
            pltpu.SemaphoreType.DMA((2, COLS)),
            pltpu.SemaphoreType.DMA((22,)),
        ],
        compiler_params=pltpu.CompilerParams(collective_id=0, has_side_effects=True, vmem_limit_bytes=32 * 1024 * 1024),
        name="exchange",
    )(fine, coarse)


def tap_pieces(parity):
    out = []
    for s in (1, 2, 3):
        if parity == 0:
            out += [(s, -1, 2, 3), (s, 0, 0, 5)]
        else:
            out += [(s, 0, 0, 5), (s, 1, 0, 3)]
    first = 0 if parity == 0 else 2
    for s in (0, 2, 4):
        for off in (-2, 0, 2):
            if s == 2 and off == 0:
                continue
            out.append((s, off, first, 3))
    return out


def local_kernel(
    where, params, fine, left, right, top, bottom, top_left, top_right, bottom_left, bottom_right, patch,
    coarse_first, coarse_second, local_weight, dilated_weight, out,
    raw, shifted, taps_raw, taps, first_taps, second_taps, hal_top, hal_low, edges, corners, lifted,
    patch_in, grid_act, grid_raw, cells1, cells2, cells3, keys1, keys2, turned, blocks, acc, staged,
    in_sem, w_sem, out_sem,
):
    f32, bf = jnp.float32, jnp.bfloat16
    r, c = where()
    ratio, lift, keep, gain = params[0], params[1], params[2], params[3]

    loads = []

    def load(src, dst, k):
        cp = pltpu.make_async_copy(src, dst, in_sem.at[k])
        cp.start()
        loads.append(cp)

    for p in range(PAIRS):
        load(fine.at[:, pl.ds(PAIR * p, PAIR)], raw.at[p + 2], p)
    for p in range(2):
        load(left.at[:, pl.ds(PAIR * p, PAIR)], raw.at[p], 32 + p)
        load(right.at[:, pl.ds(PAIR * p, PAIR)], raw.at[34 + p], 34 + p)
    load(top, edges.at[0], 36)
    load(bottom, edges.at[1], 37)
    for k, ref in enumerate((top_left, top_right, bottom_left, bottom_right)):
        load(ref, corners.at[k], 38 + k)
    load(patch, patch_in, 42)
    w_loads = []
    for k, ref in enumerate((dilated_weight, local_weight, coarse_first, coarse_second)):
        cp = pltpu.make_async_copy(ref, taps_raw.at[k], w_sem.at[k])
        cp.start()
        w_loads.append(cp)
    for cp in loads:
        cp.wait()

    hal_top[...] = jnp.zeros_like(hal_top)
    hal_low[...] = jnp.zeros_like(hal_low)
    for slot, ref, base in ((0, hal_top, 4), (1, hal_low, 0)):
        for p in range(PAIRS):
            g, q = p // 8, p % 8
            block = edges[slot, :, PAIR * q : PAIR * (q + 1)].astype(f32)
            ref[p + 2, base : base + 4, :] = block[4 * g : 4 * g + 4]
    for p in range(2):
        lanes = slice(PAIR * p, PAIR * (p + 1))
        hal_top[p, 4:8, :] = corners[0, :, lanes].astype(f32)[12:16]
        hal_top[34 + p, 4:8, :] = corners[1, :, lanes].astype(f32)[12:16]
        hal_low[p, 0:4, :] = corners[2, :, lanes].astype(f32)[0:4]
        hal_low[34 + p, 0:4, :] = corners[3, :, lanes].astype(f32)[0:4]

    def prepare(p, _):
        lifted[0:8, :] = silu(hal_top[p])
        lifted[8:72, :] = silu(raw[p].astype(f32))
        lifted[72:80, :] = silu(hal_low[p])
        for k, s in enumerate(SHIFTS):
            shifted[k, p] = lifted[8 + s : 72 + s, :].astype(bf)
        return 0

    lax.fori_loop(0, PAIRS + 4, prepare, 0)

    for cp in w_loads:
        cp.wait()
    gap = jnp.zeros((C, 64), bf)
    dilated = lambda a, b: taps_raw[0, 3 * a + b]
    local = lambda a, b: (ratio * taps_raw[1, 3 * a + b].astype(f32)).astype(bf)
    for par in range(2):
        at = 0
        for a in range(3):
            row = []
            for b in range(3):
                if a == 1 and b == 1:
                    row.append((dilated(1, 1).astype(f32) + ratio * taps_raw[1, 4].astype(f32)).astype(bf))
                else:
                    row.append(local(a, b))
            row = [gap] + row if par == 0 else row + [gap]
            taps[par, :, at : at + 1024] = jnp.concatenate(row, axis=1)
            at += 1024
        for a in range(3):
            for b in range(3):
                if a == 1 and b == 1:
                    continue
                w = dilated(a, b)
                taps[par, :, at : at + 384] = jnp.concatenate([w, gap] if par == 0 else [gap, w], axis=1)
                at += 384
    for k in range(9):
        first_taps[:, 384 * k : 384 * k + 384] = jnp.concatenate([taps_raw[2, k], gap], axis=1)
        second_taps[:, 384 * k : 384 * k + 384] = jnp.concatenate([taps_raw[3, k], gap], axis=1)
    eye = lax.broadcasted_iota(jnp.int32, (C, 384), 0) == lax.broadcasted_iota(jnp.int32, (C, 384), 1)
    second_taps[:, 3456:3840] = eye.astype(f32).astype(bf)

    values = patch_in[...].astype(f32).reshape(22 * 32, 384)
    for t in range(3):
        part = values[:, 128 * t : 128 * t + 128]
        grid_raw[t] = part
        grid_act[t] = silu(part)
    cells1[...] = jnp.zeros_like(cells1)
    cells2[...] = jnp.zeros_like(cells2)
    cells3[...] = jnp.zeros_like(cells3)
    for t in range(3):
        lanes = slice(128 * t, 128 * t + 128)
        for m in range(22):
            cells1[24 * m : 24 * m + 22, lanes] = grid_act[t, pl.ds(m + 1, 22, stride=32), :]
        for m in range(18):
            cells3[PITCH * m : PITCH * m + PITCH, lanes] = grid_raw[t, pl.ds(64 + m + 3, PITCH, stride=32), :]
    for a in range(3):
        for b in range(3):
            k = 3 * a + b
            first = 24 * b + a
            keys1[:, 384 * k : 384 * k + 384] = cells1[first : first + 512, :].astype(bf)
    contract = (((1,), (1,)), ((), ()))
    hidden = lax.dot_general(first_taps[...], keys1[...], contract, preferred_element_type=f32)
    hidden = jnp.concatenate([silu(hidden), jnp.zeros((64, 512), f32)], axis=0)
    turned[...] = jnp.transpose(hidden)
    field_row = lax.broadcasted_iota(jnp.int32, (PITCH, 384), 0) + (16 * r - 2)
    row_ok = jnp.logical_and(field_row >= 0, field_row < 128)
    for m in range(20):
        col = 16 * c - 2 + m
        ok = jnp.logical_and(row_ok, jnp.logical_and(col >= 0, col < 256))
        cells2[PITCH * m : PITCH * m + PITCH, :] = jnp.where(ok, turned[24 * m : 24 * m + PITCH, :], 0.0)
    for a in range(3):
        for b in range(3):
            k = 3 * a + b
            first = PITCH * b + a
            keys2[:, 384 * k : 384 * k + 384] = cells2[first : first + 384, :].astype(bf)
    keys2[:, 3456:3840] = cells3[...].astype(bf)
    coarse = lift * lax.dot_general(second_taps[...], keys2[...], contract, preferred_element_type=f32)
    for q in range(4):
        part = coarse if q == 0 else pltpu.roll(coarse, 384 - 80 * q, axis=1)
        part = part[:, 0:128]
        high = part.astype(bf)
        blocks[q, :, 0:128] = high
        blocks[q, :, 128:256] = (part - high.astype(f32)).astype(bf)

    lane = lax.broadcasted_iota(jnp.int32, (TALL, 128), 1)
    group = jnp.zeros((TALL, 128), jnp.int32)
    for t in range(1, 7):
        group = group + (lane >= PITCH * t).astype(jnp.int32)
    lane_row = (lane - PITCH * group + (16 * r - 1)).astype(f32)
    lane_col = (group + (16 * c - 1)).astype(f32)
    fine_row = (lax.broadcasted_iota(jnp.int32, (TALL, 128), 0) + 64 * r).astype(f32)
    where_row = jnp.clip((fine_row + 0.5) * 0.25 - 0.5, 0.0, 127.0)
    row_share = jnp.maximum(1.0 - jnp.abs(where_row - lane_row), 0.0)
    base_col = (jnp.zeros((TALL, 128), jnp.int32) + 64 * c).astype(f32)

    def shares(q, par):
        out = []
        for pp in range(CHUNK):
            spot = jnp.clip((base_col + (16 * q + 2 * pp + par + 0.5)) * 0.25 - 0.5, 0.0, 255.0)
            part = row_share * jnp.maximum(1.0 - jnp.abs(spot - (lane_col + 4 * q)), 0.0)
            out.append(jnp.concatenate([part, part], axis=1).astype(bf))
        return jnp.concatenate(out, axis=0)

    pending = [None, None]
    for q in range(4):
        for par in range(2):
            pieces = []
            for s, off, tile, n in tap_pieces(par):
                first = 2 + CHUNK * q + off
                part = shifted[s, first : first + CHUNK, :, 128 * tile : 128 * (tile + n)]
                pieces.append(part.reshape(CELLS, 128 * n))
            pieces.append(shares(q, par))
            rhs = jnp.concatenate(pieces, axis=1)
            lhs = jnp.concatenate([taps[par], blocks[q]], axis=1)
            acc[C * par : C * par + C, :] = lax.dot_general(lhs, rhs, contract, preferred_element_type=f32)
        slot = q % 2
        if pending[slot] is not None:
            pending[slot].wait()
        for u in range(CHUNK // 2):
            block = jnp.transpose(acc[:, 128 * u : 128 * u + 128])
            for v in range(2):
                pp = 2 * u + v
                cells = raw[2 + CHUNK * q + pp].astype(f32)
                staged[slot, :, PAIR * pp : PAIR * (pp + 1)] = keep * cells + gain * block[64 * v : 64 * v + 64]
        cp = pltpu.make_async_copy(staged.at[slot], out.at[:, pl.ds(5120 * q, 5120)], out_sem.at[slot])
        cp.start()
        pending[slot] = cp
    for cp in pending:
        cp.wait()


def local_work(where, params, *arrays):
    f32, bf = jnp.float32, jnp.bfloat16
    any_spec = pl.BlockSpec(memory_space=pl.ANY)
    return pl.pallas_call(
        functools.partial(local_kernel, where),
        out_shape=jax.ShapeDtypeStruct((64, 20480), f32),
        in_specs=[pl.BlockSpec(memory_space=pltpu.SMEM)] + [any_spec] * len(arrays),
        out_specs=any_spec,
        scratch_shapes=[
            pltpu.VMEM((36, 64, 640), bf),
            pltpu.VMEM((5, 36, 64, 640), bf),
            pltpu.VMEM((4, 9, C, C), bf),
            pltpu.VMEM((2, C, KEYS), bf),
            pltpu.VMEM((C, 3456), bf),
            pltpu.VMEM((C, 3840), bf),
            pltpu.VMEM((36, 8, 640), f32),
            pltpu.VMEM((36, 8, 640), f32),
            pltpu.VMEM((2, 16, 5120), bf),
            pltpu.VMEM((4, 16, 1280), bf),
            pltpu.VMEM((80, 640), f32),
            pltpu.VMEM((22, 32, 384), bf),
            pltpu.VMEM((3, 704, 128), f32),
            pltpu.VMEM((3, 704, 128), f32),
            pltpu.VMEM((568, 384), f32),
            pltpu.VMEM((432, 384), f32),
            pltpu.VMEM((384, 384), f32),
            pltpu.VMEM((512, 3456), bf),
            pltpu.VMEM((384, 3840), bf),
            pltpu.VMEM((512, 384), f32),
            pltpu.VMEM((4, C, 256), bf),
            pltpu.VMEM((PAIR, CELLS), f32),
            pltpu.VMEM((2, 64, 5120), f32),
            pltpu.SemaphoreType.DMA((43,)),
            pltpu.SemaphoreType.DMA((4,)),
            pltpu.SemaphoreType.DMA((2,)),
        ],
        compiler_params=pltpu.CompilerParams(vmem_limit_bytes=VMEM_LIMIT),
        name="local_work",
    )(params, *arrays)


def blend_params(timestep):
    mix = (1.0 + jnp.cos(math.pi * timestep[0].astype(jnp.float32) / STEPS)) / 2.0
    skip = mix**3
    gain = (1.0 - skip) * mix
    return jnp.stack([(1.0 - mix) / mix, skip / gain, 1.0 - skip, gain])


def on_device(coarse_latent, fine_latent, timestep, coarse_first, coarse_second, local_weight, dilated_weight):
    row = jnp.transpose(coarse_latent.reshape(C, 256))
    row = jnp.pad(row, ((4, 28), (0, 64)))
    halos = exchange(fine_latent, row)
    flat = lambda w: w.reshape(9, C, C)
    return local_work(
        lambda: (lax.axis_index("row"), lax.axis_index("col")),
        blend_params(timestep), fine_latent, *halos,
        flat(coarse_first), flat(coarse_second), flat(local_weight), flat(dilated_weight))


def solution(mesh):
    placed = (P(None, ("row", "col"), None), P("row", "col"), P(), P(), P(), P(), P())
    return jax.shard_map(
        on_device, mesh=mesh, in_specs=placed, out_specs=P("row", "col"), check_vma=False
    )
```

```python
import functools
import math

import jax
import jax.numpy as jnp
from jax import lax
from jax.experimental import pallas as pl
from jax.experimental.pallas import tpu as pltpu
from jax.sharding import PartitionSpec as P

STEPS = 50
C = 320
ROWS = 8
COLS = 16
PAIR = 2 * C
TALL = 64
PAIRS = 32
CHUNK = 8
CELLS = CHUNK * TALL
SHIFTS = (-4, -1, 0, 1, 4)
KEYS = 6144
PITCH = 20
MESH = pl.DeviceIdType.MESH
VMEM_LIMIT = 60 * 1024 * 1024


def silu(x):
    return x / (1.0 + jnp.exp(-x))


def tap_pieces(parity):
    out = []
    for s in (1, 2, 3):
        if parity == 0:
            out += [(s, -1, 2, 3), (s, 0, 0, 5)]
        else:
            out += [(s, 0, 0, 5), (s, 1, 0, 3)]
    first = 0 if parity == 0 else 2
    for s in (0, 2, 4):
        for off in (-2, 0, 2):
            if s == 2 and off == 0:
                continue
            out.append((s, off, first, 3))
    return out


def whole_kernel(
    timestep, fine, coarse_row, coarse_first, coarse_second, local_weight, dilated_weight, out,
    raw, shifted, taps_raw, taps, first_taps, second_taps, hal_top, hal_low, packed, edges, corners, lifted,
    row_in, window_row, patch_in, grid_act, grid_raw, cells1, cells2, cells3, keys1, keys2, turned, blocks, acc, staged,
    in_sem, w_sem, out_sem, send_sem, recv_sem, patch_send, patch_recv,
):
    f32, bf = jnp.float32, jnp.bfloat16
    r = lax.axis_index("row")
    c = lax.axis_index("col")
    above = r > 0
    below = r < ROWS - 1
    down = jnp.logical_and(below, c >= 13)
    up = jnp.logical_and(above, c < 3)

    def present(dr, dc):
        ok = None
        for cond, need in ((above, dr < 0), (below, dr > 0), (c > 0, dc < 0), (c < COLS - 1, dc > 0)):
            if need:
                ok = cond if ok is None else jnp.logical_and(ok, cond)
        return ok

    barrier = pltpu.get_barrier_semaphore()

    def greet(dev):
        pl.semaphore_signal(barrier, inc=1, device_id=dev, device_id_type=MESH)

    def greet_row(step, _):
        greet((r, lax.rem(c + step, COLS)))
        return 0

    lax.fori_loop(1, COLS, greet_row, 0)
    diagonal = ((-1, -1), (-1, 0), (-1, 1), (1, -1), (1, 0), (1, 1))
    expected = COLS - 1 + jnp.where(down, COLS, 0) + jnp.where(up, COLS, 0)
    for step in diagonal:
        @pl.when(present(*step))
        def _(step=step):
            greet((r + step[0], c + step[1]))
        expected = expected + jnp.where(present(*step), 1, 0)
    for k in range(3):
        @pl.when(above)
        def _(k=k):
            greet((r - 1, 13 + k))

        @pl.when(below)
        def _(k=k):
            greet((r + 1, k))

    row_load = pltpu.make_async_copy(coarse_row, row_in, in_sem.at[PAIRS])
    row_load.start()
    loads = []
    for p in range(PAIRS):
        cp = pltpu.make_async_copy(fine.at[:, pl.ds(PAIR * p, PAIR)], raw.at[p + 2], in_sem.at[p])
        cp.start()
        loads.append(cp)
    w_loads = []
    for k, ref in enumerate((dilated_weight, local_weight, coarse_first, coarse_second)):
        cp = pltpu.make_async_copy(ref, taps_raw.at[k], w_sem.at[k])
        cp.start()
        w_loads.append(cp)

    side_zero = jnp.zeros((2, TALL, PAIR), bf)

    @pl.when(c == 0)
    def _():
        raw[0:2] = side_zero
        corners[0] = jnp.zeros((2, 16, PAIR), bf)
        corners[2] = jnp.zeros((2, 16, PAIR), bf)

    @pl.when(c == COLS - 1)
    def _():
        raw[34:36] = side_zero
        corners[1] = jnp.zeros((2, 16, PAIR), bf)
        corners[3] = jnp.zeros((2, 16, PAIR), bf)

    @pl.when(jnp.logical_not(above))
    def _():
        edges[0] = jnp.zeros((8, 16, PAIR), bf)
        corners[0] = jnp.zeros((2, 16, PAIR), bf)
        corners[1] = jnp.zeros((2, 16, PAIR), bf)
        patch_in[0:3] = jnp.zeros((3, 32, 384), bf)

    @pl.when(jnp.logical_not(below))
    def _():
        edges[1] = jnp.zeros((8, 16, PAIR), bf)
        corners[2] = jnp.zeros((2, 16, PAIR), bf)
        corners[3] = jnp.zeros((2, 16, PAIR), bf)
        patch_in[19:22] = jnp.zeros((3, 32, 384), bf)

    row_load.wait()
    turned_row = jnp.concatenate([row_in[...].astype(f32), jnp.zeros((64, 256), f32)], axis=0)
    acc[0:256, 0:384] = jnp.transpose(turned_row)
    window_row[...] = jnp.concatenate(
        [jnp.zeros((4, 384), f32), acc[0:256, 0:384], jnp.zeros((28, 384), f32)], axis=0).astype(bf)
    for cp in loads:
        cp.wait()
    for slot, first in ((0, 0), (1, 12)):
        for q in range(8):
            rows = []
            for g in range(4):
                base = 0 if slot == 0 else 48
                rows.append(raw[2 + 8 * g + q, base : base + 16, :].astype(f32)[first : first + 4])
            packed[slot, q] = jnp.concatenate(rows, axis=0).astype(bf)
    pl.semaphore_wait(barrier, expected)

    last = pl.ds(32, 2)
    head = pl.ds(2, 2)
    upper, lower = pl.ds(0, 16), pl.ds(48, 16)
    sides = (
        ((0, 1), raw.at[last], raw.at[pl.ds(0, 2)]),
        ((0, -1), raw.at[head], raw.at[pl.ds(34, 2)]),
        ((1, 0), packed.at[1], edges.at[0]),
        ((-1, 0), packed.at[0], edges.at[1]),
        ((1, 1), raw.at[last, lower], corners.at[0]),
        ((1, -1), raw.at[head, lower], corners.at[1]),
        ((-1, 1), raw.at[last, upper], corners.at[2]),
        ((-1, -1), raw.at[head, upper], corners.at[3]),
    )

    def side_copy(k):
        step, src, dst = sides[k]
        return pltpu.make_async_remote_copy(
            src_ref=src, dst_ref=dst, send_sem=send_sem.at[k], recv_sem=recv_sem.at[k],
            device_id=(r + step[0], c + step[1]), device_id_type=MESH)

    for k in range(8):
        @pl.when(present(*sides[k][0]))
        def _(k=k):
            side_copy(k).start()

    def window(target):
        return window_row.at[pl.ds(pl.multiple_of(16 * target, 16), 32), :]

    def patch_copy(dev_r, dev_c, k, slot):
        return pltpu.make_async_remote_copy(
            src_ref=window(dev_c), dst_ref=patch_in.at[k], send_sem=patch_send.at[slot, dev_c],
            recv_sem=patch_recv.at[k], device_id=(dev_r, dev_c), device_id_type=MESH)

    own = pltpu.make_async_copy(window(c), patch_in.at[c + 3], patch_recv.at[c + 3])
    own.start()

    def send_row(step, _):
        patch_copy(r, lax.rem(c + step, COLS), c + 3, 0).start()
        return 0

    lax.fori_loop(1, COLS, send_row, 0)

    @pl.when(down)
    def _():
        def one(step, _):
            patch_copy(r + 1, lax.rem(c + step, COLS), c - 13, 1).start()
            return 0
        lax.fori_loop(0, COLS, one, 0)

    @pl.when(up)
    def _():
        def one(step, _):
            patch_copy(r - 1, lax.rem(c + step, COLS), c + 19, 1).start()
            return 0
        lax.fori_loop(0, COLS, one, 0)

    angle = jnp.full((8, 128), timestep[0].astype(f32) * (math.pi / STEPS), f32)
    mix_all = (1.0 + jnp.cos(angle)) * 0.5
    skip_all = mix_all * mix_all * mix_all
    gain_all = (1.0 - skip_all) * mix_all
    one_of = lambda v: v[0:1, 0:1]
    ratio, lift = one_of((1.0 - mix_all) / mix_all), one_of(skip_all / gain_all)
    keep, gain = one_of(1.0 - skip_all), one_of(gain_all)

    for cp in w_loads:
        cp.wait()
    gap = jnp.zeros((C, 64), bf)
    dilated = lambda a, b: taps_raw[0, 3 * a + b]
    local = lambda a, b: (ratio * taps_raw[1, 3 * a + b].astype(f32)).astype(bf)
    for par in range(2):
        at = 0
        for a in range(3):
            row = []
            for b in range(3):
                if a == 1 and b == 1:
                    row.append((dilated(1, 1).astype(f32) + ratio * taps_raw[1, 4].astype(f32)).astype(bf))
                else:
                    row.append(local(a, b))
            row = [gap] + row if par == 0 else row + [gap]
            taps[par, :, at : at + 1024] = jnp.concatenate(row, axis=1)
            at += 1024
        for a in range(3):
            for b in range(3):
                if a == 1 and b == 1:
                    continue
                w = dilated(a, b)
                taps[par, :, at : at + 384] = jnp.concatenate([w, gap] if par == 0 else [gap, w], axis=1)
                at += 384
    for k in range(9):
        first_taps[:, 384 * k : 384 * k + 384] = jnp.concatenate([taps_raw[2, k], gap], axis=1)
        second_taps[:, 384 * k : 384 * k + 384] = jnp.concatenate([taps_raw[3, k], gap], axis=1)
    eye = lax.broadcasted_iota(jnp.int32, (C, 384), 0) == lax.broadcasted_iota(jnp.int32, (C, 384), 1)
    second_taps[:, 3456:3840] = eye.astype(f32).astype(bf)

    for k in range(8):
        step, src, dst = sides[k]
        @pl.when(present(-step[0], -step[1]))
        def _(k=k):
            side_copy(k).wait_recv()

    hal_top[...] = jnp.zeros_like(hal_top)
    hal_low[...] = jnp.zeros_like(hal_low)
    for slot, ref, base in ((0, hal_top, 4), (1, hal_low, 0)):
        for q in range(8):
            block = edges[slot, q].astype(f32)
            for g in range(4):
                ref[2 + 8 * g + q, base : base + 4, :] = block[4 * g : 4 * g + 4]
    for p in range(2):
        hal_top[p, 4:8, :] = corners[0, p].astype(f32)[12:16]
        hal_top[34 + p, 4:8, :] = corners[1, p].astype(f32)[12:16]
        hal_low[p, 0:4, :] = corners[2, p].astype(f32)[0:4]
        hal_low[34 + p, 0:4, :] = corners[3, p].astype(f32)[0:4]

    def prepare(p, _):
        lifted[0:8, :] = silu(hal_top[p])
        lifted[8:72, :] = silu(raw[p].astype(f32))
        lifted[72:80, :] = silu(hal_low[p])
        for k, s in enumerate(SHIFTS):
            shifted[k, p] = lifted[8 + s : 72 + s, :].astype(bf)
        return 0

    lax.fori_loop(0, PAIRS + 4, prepare, 0)

    own.wait()

    def got_row(step, _):
        k = lax.rem(c + step, COLS) + 3
        pltpu.make_async_copy(window_row.at[pl.ds(0, 32), :], patch_in.at[k], patch_recv.at[k]).wait()
        return 0

    lax.fori_loop(1, COLS, got_row, 0)
    for k in range(3):
        for cond, slot in ((above, k), (below, 19 + k)):
            @pl.when(cond)
            def _(slot=slot):
                pltpu.make_async_copy(window_row.at[pl.ds(0, 32), :], patch_in.at[slot], patch_recv.at[slot]).wait()

    values = patch_in[...].astype(f32).reshape(22 * 32, 384)
    for t in range(3):
        part = values[:, 128 * t : 128 * t + 128]
        grid_raw[t] = part
        grid_act[t] = silu(part)
    cells1[...] = jnp.zeros_like(cells1)
    cells2[...] = jnp.zeros_like(cells2)
    cells3[...] = jnp.zeros_like(cells3)
    for t in range(3):
        lanes = slice(128 * t, 128 * t + 128)
        for m in range(22):
            cells1[24 * m : 24 * m + 22, lanes] = grid_act[t, pl.ds(m + 1, 22, stride=32), :]
        for m in range(18):
            cells3[PITCH * m : PITCH * m + PITCH, lanes] = grid_raw[t, pl.ds(64 + m + 3, PITCH, stride=32), :]
    for a in range(3):
        for b in range(3):
            k = 3 * a + b
            first = 24 * b + a
            keys1[:, 384 * k : 384 * k + 384] = cells1[first : first + 512, :].astype(bf)
    contract = (((1,), (1,)), ((), ()))
    hidden = lax.dot_general(first_taps[...], keys1[...], contract, preferred_element_type=f32)
    hidden = jnp.concatenate([silu(hidden), jnp.zeros((64, 512), f32)], axis=0)
    turned[...] = jnp.transpose(hidden)
    field_row = lax.broadcasted_iota(jnp.int32, (PITCH, 384), 0) + (16 * r - 2)
    row_ok = jnp.logical_and(field_row >= 0, field_row < 128)
    for m in range(20):
        col = 16 * c - 2 + m
        ok = jnp.logical_and(row_ok, jnp.logical_and(col >= 0, col < 256))
        cells2[PITCH * m : PITCH * m + PITCH, :] = jnp.where(ok, turned[24 * m : 24 * m + PITCH, :], 0.0)
    for a in range(3):
        for b in range(3):
            k = 3 * a + b
            first = PITCH * b + a
            keys2[:, 384 * k : 384 * k + 384] = cells2[first : first + 384, :].astype(bf)
    keys2[:, 3456:3840] = cells3[...].astype(bf)
    coarse = lift * lax.dot_general(second_taps[...], keys2[...], contract, preferred_element_type=f32)
    for q in range(4):
        part = coarse if q == 0 else pltpu.roll(coarse, 384 - 80 * q, axis=1)
        part = part[:, 0:128]
        high = part.astype(bf)
        blocks[q, :, 0:128] = high
        blocks[q, :, 128:256] = (part - high.astype(f32)).astype(bf)

    lane = lax.broadcasted_iota(jnp.int32, (TALL, 128), 1)
    group = jnp.zeros((TALL, 128), jnp.int32)
    for t in range(1, 7):
        group = group + (lane >= PITCH * t).astype(jnp.int32)
    lane_row = (lane - PITCH * group + (16 * r - 1)).astype(f32)
    lane_col = (group + (16 * c - 1)).astype(f32)
    fine_row = (lax.broadcasted_iota(jnp.int32, (TALL, 128), 0) + 64 * r).astype(f32)
    where_row = jnp.clip((fine_row + 0.5) * 0.25 - 0.5, 0.0, 127.0)
    row_share = jnp.maximum(1.0 - jnp.abs(where_row - lane_row), 0.0)
    base_col = (jnp.zeros((TALL, 128), jnp.int32) + 64 * c).astype(f32)

    def shares(q, par):
        out = []
        for pp in range(CHUNK):
            spot = jnp.clip((base_col + (16 * q + 2 * pp + par + 0.5)) * 0.25 - 0.5, 0.0, 255.0)
            part = row_share * jnp.maximum(1.0 - jnp.abs(spot - (lane_col + 4 * q)), 0.0)
            out.append(jnp.concatenate([part, part], axis=1).astype(bf))
        return jnp.concatenate(out, axis=0)

    pending = [None, None]
    for q in range(4):
        for par in range(2):
            pieces = []
            for s, off, tile, n in tap_pieces(par):
                first = 2 + CHUNK * q + off
                part = shifted[s, first : first + CHUNK, :, 128 * tile : 128 * (tile + n)]
                pieces.append(part.reshape(CELLS, 128 * n))
            pieces.append(shares(q, par))
            rhs = jnp.concatenate(pieces, axis=1)
            lhs = jnp.concatenate([taps[par], blocks[q]], axis=1)
            acc[C * par : C * par + C, :] = lax.dot_general(lhs, rhs, contract, preferred_element_type=f32)
        slot = q % 2
        if pending[slot] is not None:
            pending[slot].wait()
        for u in range(CHUNK // 2):
            block = jnp.transpose(acc[:, 128 * u : 128 * u + 128])
            for v in range(2):
                pp = 2 * u + v
                cells = raw[2 + CHUNK * q + pp].astype(f32)
                staged[slot, :, PAIR * pp : PAIR * (pp + 1)] = keep * cells + gain * block[64 * v : 64 * v + 64]
        cp = pltpu.make_async_copy(staged.at[slot], out.at[:, pl.ds(5120 * q, 5120)], out_sem.at[slot])
        cp.start()
        pending[slot] = cp
    for cp in pending:
        cp.wait()

    for k in range(8):
        @pl.when(present(*sides[k][0]))
        def _(k=k):
            side_copy(k).wait_send()

    def sent_row(step, _):
        patch_copy(r, lax.rem(c + step, COLS), c + 3, 0).wait_send()
        return 0

    lax.fori_loop(1, COLS, sent_row, 0)

    @pl.when(down)
    def _():
        def one(step, _):
            patch_copy(r + 1, lax.rem(c + step, COLS), c - 13, 1).wait_send()
            return 0
        lax.fori_loop(0, COLS, one, 0)

    @pl.when(up)
    def _():
        def one(step, _):
            patch_copy(r - 1, lax.rem(c + step, COLS), c + 19, 1).wait_send()
            return 0
        lax.fori_loop(0, COLS, one, 0)


def whole(*arrays):
    f32, bf = jnp.float32, jnp.bfloat16
    any_spec = pl.BlockSpec(memory_space=pl.ANY)
    return pl.pallas_call(
        whole_kernel,
        out_shape=jax.ShapeDtypeStruct((64, 20480), f32),
        in_specs=[pl.BlockSpec(memory_space=pltpu.SMEM)] + [any_spec] * 6,
        out_specs=any_spec,
        scratch_shapes=[
            pltpu.VMEM((36, 64, 640), bf),
            pltpu.VMEM((5, 36, 64, 640), bf),
            pltpu.VMEM((4, 9, C, C), bf),
            pltpu.VMEM((2, C, KEYS), bf),
            pltpu.VMEM((C, 3456), bf),
            pltpu.VMEM((C, 3840), bf),
            pltpu.VMEM((36, 8, 640), f32),
            pltpu.VMEM((36, 8, 640), f32),
            pltpu.VMEM((2, 8, 16, 640), bf),
            pltpu.VMEM((2, 8, 16, 640), bf),
            pltpu.VMEM((4, 2, 16, 640), bf),
            pltpu.VMEM((80, 640), f32),
            pltpu.VMEM((C, 256), bf),
            pltpu.VMEM((288, 384), bf),
            pltpu.VMEM((22, 32, 384), bf),
            pltpu.VMEM((3, 704, 128), f32),
            pltpu.VMEM((3, 704, 128), f32),
            pltpu.VMEM((568, 384), f32),
            pltpu.VMEM((432, 384), f32),
            pltpu.VMEM((384, 384), f32),
            pltpu.VMEM((512, 3456), bf),
            pltpu.VMEM((384, 3840), bf),
            pltpu.VMEM((512, 384), f32),
            pltpu.VMEM((4, C, 256), bf),
            pltpu.VMEM((PAIR, CELLS), f32),
            pltpu.VMEM((2, 64, 5120), f32),
            pltpu.SemaphoreType.DMA((PAIRS + 1,)),
            pltpu.SemaphoreType.DMA((4,)),
            pltpu.SemaphoreType.DMA((2,)),
            pltpu.SemaphoreType.DMA((8,)),
            pltpu.SemaphoreType.DMA((8,)),
            pltpu.SemaphoreType.DMA((2, COLS)),
            pltpu.SemaphoreType.DMA((22,)),
        ],
        compiler_params=pltpu.CompilerParams(collective_id=0, has_side_effects=True, vmem_limit_bytes=VMEM_LIMIT),
        name="whole",
    )(*arrays)


def on_device(coarse_latent, fine_latent, timestep, coarse_first, coarse_second, local_weight, dilated_weight):
    flat = lambda w: w.reshape(9, C, C)
    return whole(
        timestep, fine_latent, coarse_latent.reshape(C, 256),
        flat(coarse_first), flat(coarse_second), flat(local_weight), flat(dilated_weight))


def solution(mesh):
    placed = (P(None, ("row", "col"), None), P("row", "col"), P(), P(), P(), P(), P())
    return jax.shard_map(
        on_device, mesh=mesh, in_specs=placed, out_specs=P("row", "col"), check_vma=False
    )
```

```python
import functools
import math

import jax
import jax.numpy as jnp
from jax import lax
from jax.experimental import pallas as pl
from jax.experimental.pallas import tpu as pltpu
from jax.sharding import PartitionSpec as P

STEPS = 50
C = 320
ROWS = 8
COLS = 16
PAIR = 2 * C
TALL = 64
PAIRS = 32
CHUNK = 16
CELLS = CHUNK * 32
SHIFTS = (-4, -1, 0, 1, 4)
KEYS = 6144
PITCH = 20
MESH = pl.DeviceIdType.MESH
VMEM_LIMIT = 60 * 1024 * 1024


def silu(x):
    return x / (1.0 + jnp.exp(-x))


def tap_pieces(parity):
    out = []
    for s in (1, 2, 3):
        if parity == 0:
            out += [(s, -1, 2, 3), (s, 0, 0, 5)]
        else:
            out += [(s, 0, 0, 5), (s, 1, 0, 3)]
    first = 0 if parity == 0 else 2
    for s in (0, 2, 4):
        for off in (-2, 0, 2):
            if s == 2 and off == 0:
                continue
            out.append((s, off, first, 3))
    return out


def whole_kernel(
    timestep, fine, coarse_row, coarse_first, coarse_second, local_weight, dilated_weight, out,
    raw, shifted, taps_raw, taps, packed, edges, corner_out, corners, row_in, window_row, patch_in, blocks, acc, staged,
    in_sem, w_sem, out_sem, send_sem, recv_sem, patch_send, patch_recv,
):
    f32, bf = jnp.float32, jnp.bfloat16
    r = lax.axis_index("row")
    c = lax.axis_index("col")
    above = r > 0
    below = r < ROWS - 1
    down = jnp.logical_and(below, c >= 13)
    up = jnp.logical_and(above, c < 3)

    def present(dr, dc):
        ok = None
        for cond, need in ((above, dr < 0), (below, dr > 0), (c > 0, dc < 0), (c < COLS - 1, dc > 0)):
            if need:
                ok = cond if ok is None else jnp.logical_and(ok, cond)
        return ok

    barrier = pltpu.get_barrier_semaphore()

    def greet(dev):
        pl.semaphore_signal(barrier, inc=1, device_id=dev, device_id_type=MESH)

    def greet_row(step, _):
        greet((r, lax.rem(c + step, COLS)))
        return 0

    lax.fori_loop(1, COLS, greet_row, 0)
    diagonal = ((-1, -1), (-1, 0), (-1, 1), (1, -1), (1, 0), (1, 1))
    expected = COLS - 1 + jnp.where(down, COLS, 0) + jnp.where(up, COLS, 0)
    for step in diagonal:
        @pl.when(present(*step))
        def _(step=step):
            greet((r + step[0], c + step[1]))
        expected = expected + jnp.where(present(*step), 1, 0)
    for k in range(3):
        @pl.when(above)
        def _(k=k):
            greet((r - 1, 13 + k))

        @pl.when(below)
        def _(k=k):
            greet((r + 1, k))

    row_load = pltpu.make_async_copy(coarse_row, row_in, in_sem.at[PAIRS])
    row_load.start()
    loads = []
    for p in range(PAIRS):
        cp = pltpu.make_async_copy(fine.at[:, pl.ds(PAIR * p, PAIR)], raw.at[p + 2], in_sem.at[p])
        cp.start()
        loads.append(cp)
    w_loads = []
    for k, ref in enumerate((dilated_weight, local_weight, coarse_first, coarse_second)):
        cp = pltpu.make_async_copy(ref, taps_raw.at[k], w_sem.at[k])
        cp.start()
        w_loads.append(cp)

    side_zero = jnp.zeros((2, TALL, PAIR), bf)

    @pl.when(c == 0)
    def _():
        raw[0:2] = side_zero
        corners[0] = jnp.zeros((16, PAIR), bf)
        corners[2] = jnp.zeros((16, PAIR), bf)

    @pl.when(c == COLS - 1)
    def _():
        raw[34:36] = side_zero
        corners[1] = jnp.zeros((16, PAIR), bf)
        corners[3] = jnp.zeros((16, PAIR), bf)

    @pl.when(jnp.logical_not(above))
    def _():
        edges[0] = jnp.zeros((8, 16, PAIR), bf)
        corners[0] = jnp.zeros((16, PAIR), bf)
        corners[1] = jnp.zeros((16, PAIR), bf)
        patch_in[0:3] = jnp.zeros((3, 32, 384), bf)

    @pl.when(jnp.logical_not(below))
    def _():
        edges[1] = jnp.zeros((8, 16, PAIR), bf)
        corners[2] = jnp.zeros((16, PAIR), bf)
        corners[3] = jnp.zeros((16, PAIR), bf)
        patch_in[19:22] = jnp.zeros((3, 32, 384), bf)

    row_load.wait()
    turned_row = jnp.concatenate([row_in[...].astype(f32), jnp.zeros((64, 256), f32)], axis=0)
    window_row[...] = jnp.concatenate(
        [jnp.zeros((4, 384), f32), jnp.transpose(turned_row), jnp.zeros((28, 384), f32)], axis=0).astype(bf)
    for cp in loads:
        cp.wait()
    for slot, base, first in ((0, 0, 0), (1, 48, 12)):
        tops = {}
        for p in range(PAIRS):
            tops[p] = raw[2 + p, base : base + 16, :].astype(f32)[first : first + 4]
        for q in range(8):
            packed[slot, q] = jnp.concatenate([tops[8 * g + q] for g in range(4)], axis=0).astype(bf)
        for k, p in ((0, 30), (1, 0)):
            spot = k if slot == 1 else 2 + k
            corner_out[spot] = jnp.concatenate([tops[p], tops[p + 1], jnp.zeros((8, PAIR), f32)], axis=0).astype(bf)
    pl.semaphore_wait(barrier, expected)

    last = pl.ds(32, 2)
    head = pl.ds(2, 2)
    sides = (
        ((0, 1), raw.at[last], raw.at[pl.ds(0, 2)]),
        ((0, -1), raw.at[head], raw.at[pl.ds(34, 2)]),
        ((1, 0), packed.at[1], edges.at[0]),
        ((-1, 0), packed.at[0], edges.at[1]),
        ((1, 1), corner_out.at[0], corners.at[0]),
        ((1, -1), corner_out.at[1], corners.at[1]),
        ((-1, 1), corner_out.at[2], corners.at[2]),
        ((-1, -1), corner_out.at[3], corners.at[3]),
    )

    def side_copy(k):
        step, src, dst = sides[k]
        return pltpu.make_async_remote_copy(
            src_ref=src, dst_ref=dst, send_sem=send_sem.at[k], recv_sem=recv_sem.at[k],
            device_id=(r + step[0], c + step[1]), device_id_type=MESH)

    for k in range(8):
        @pl.when(present(*sides[k][0]))
        def _(k=k):
            side_copy(k).start()

    def window(target):
        return window_row.at[pl.ds(pl.multiple_of(16 * target, 16), 32), :]

    def patch_copy(dev_r, dev_c, k, slot):
        return pltpu.make_async_remote_copy(
            src_ref=window(dev_c), dst_ref=patch_in.at[k], send_sem=patch_send.at[slot, dev_c],
            recv_sem=patch_recv.at[k], device_id=(dev_r, dev_c), device_id_type=MESH)

    own = pltpu.make_async_copy(window(c), patch_in.at[c + 3], patch_recv.at[c + 3])
    own.start()

    def send_row(step, _):
        patch_copy(r, lax.rem(c + step, COLS), c + 3, 0).start()
        return 0

    lax.fori_loop(1, COLS, send_row, 0)

    @pl.when(down)
    def _():
        def one(step, _):
            patch_copy(r + 1, lax.rem(c + step, COLS), c - 13, 1).start()
            return 0
        lax.fori_loop(0, COLS, one, 0)

    @pl.when(up)
    def _():
        def one(step, _):
            patch_copy(r - 1, lax.rem(c + step, COLS), c + 19, 1).start()
            return 0
        lax.fori_loop(0, COLS, one, 0)

    angle = jnp.full((8, 128), timestep[0].astype(f32) * (math.pi / STEPS), f32)
    mix_all = (1.0 + jnp.cos(angle)) * 0.5
    skip_all = mix_all * mix_all * mix_all
    gain_all = (1.0 - skip_all) * mix_all
    one_of = lambda v: v[0:1, 0:1]
    ratio, lift = one_of((1.0 - mix_all) / mix_all), one_of(skip_all / gain_all)
    keep, gain = one_of(1.0 - skip_all), one_of(gain_all)

    for cp in w_loads:
        cp.wait()
    gap = jnp.zeros((C, 64), bf)
    dilated = lambda a, b: taps_raw[0, 3 * a + b]
    local = lambda a, b: (ratio * taps_raw[1, 3 * a + b].astype(f32)).astype(bf)
    for par in range(2):
        at = 0
        for a in range(3):
            row = []
            for b in range(3):
                if a == 1 and b == 1:
                    row.append((dilated(1, 1).astype(f32) + ratio * taps_raw[1, 4].astype(f32)).astype(bf))
                else:
                    row.append(local(a, b))
            row = [gap] + row if par == 0 else row + [gap]
            taps[par, :, at : at + 1024] = jnp.concatenate(row, axis=1)
            at += 1024
        for a in range(3):
            for b in range(3):
                if a == 1 and b == 1:
                    continue
                w = dilated(a, b)
                taps[par, :, at : at + 384] = jnp.concatenate([w, gap] if par == 0 else [gap, w], axis=1)
                at += 384
    contract = (((1,), (1,)), ((), ()))

    lane = lax.broadcasted_iota(jnp.int32, (TALL, 256), 1)
    group = jnp.zeros((TALL, 256), jnp.int32)
    for t in range(1, 13):
        group = group + (lane >= PITCH * t).astype(jnp.int32)
    lane_row = (lane - PITCH * group + (16 * r - 1)).astype(f32)
    lane_col = (group[0:8] + (16 * c - 1)).astype(f32)
    fine_row = (lax.broadcasted_iota(jnp.int32, (TALL, 256), 0) + 64 * r).astype(f32)
    where_row = jnp.clip((fine_row + 0.5) * 0.25 - 0.5, 0.0, 127.0)
    row_share = jnp.maximum(1.0 - jnp.abs(where_row - lane_row), 0.0)
    base_col = (jnp.zeros((8, 256), jnp.int32) + 64 * c).astype(f32)
    inner = row_share[16:48].reshape(4, 8, 256)
    outer = jnp.concatenate([row_share[0:16], row_share[48:64]], axis=0).reshape(4, 8, 256)

    def shares(h, par, rim):
        out = []
        for pp in range(CHUNK):
            spot = jnp.clip((base_col + (32 * h + 2 * pp + par + 0.5)) * 0.25 - 0.5, 0.0, 255.0)
            col_share = jnp.maximum(1.0 - jnp.abs(spot - (lane_col + 8 * h)), 0.0)
            part = ((outer if rim else inner) * col_share[None]).reshape(32, 256)
            out.append(jnp.concatenate([part, part], axis=1).astype(bf))
        return jnp.concatenate(out, axis=0)

    def keys_of(h, par, rim):
        pieces = []
        for s, off, tile, n in tap_pieces(par):
            cells = pl.ds(2 + CHUNK * h + off, CHUNK)
            lanes = slice(128 * tile, 128 * (tile + n))
            if rim:
                part = jnp.concatenate([shifted[s, cells, 0:16, lanes], shifted[s, cells, 48:64, lanes]], axis=1)
            else:
                part = shifted[s, cells, 16:48, lanes]
            pieces.append(part.reshape(CELLS, 128 * n))
        return pieces

    def arrived(k):
        step = sides[k][0]

        @pl.when(present(-step[0], -step[1]))
        def _():
            side_copy(k).wait_recv()

    def fine_work(lifted):
        def first_part(p, _):
            values = silu(raw[p].astype(f32))
            lifted[p, 8:72, :] = values
            shifted[2, p] = values.astype(bf)
            for k in (0, 1, 3, 4):
                s = SHIFTS[k]
                shifted[k, p, 16:48, :] = lifted[p, 24 + s : 56 + s, :].astype(bf)
            return 0

        lax.fori_loop(2, PAIRS + 2, first_part, 0)
        arrived(0)
        arrived(1)
        for p in (0, 1, 34, 35):
            first_part(p, 0)
        for h in range(2):
            for par in range(2):
                rhs = jnp.concatenate(keys_of(h, par, False), axis=1)
                acc[h, C * par : C * par + C, :] = lax.dot_general(taps[par], rhs, contract, preferred_element_type=f32)
        for k in range(2, 8):
            arrived(k)
        for slot, base in ((0, 4), (1, 72)):
            for q in range(8):
                block = silu(edges[slot, q].astype(f32))
                for g in range(4):
                    lifted[2 + 8 * g + q, base : base + 4, :] = block[4 * g : 4 * g + 4]
            for k, first in ((0, 0), (1, 34)):
                block = silu(corners[2 * slot + k].astype(f32))
                for p in range(2):
                    lifted[first + p, base : base + 4, :] = block[4 * p : 4 * p + 4]

        def second_part(p, _):
            for k in (0, 1, 3, 4):
                s = SHIFTS[k]
                shifted[k, p, 0:16, :] = lifted[p, 8 + s : 24 + s, :].astype(bf)
                shifted[k, p, 48:64, :] = lifted[p, 56 + s : 72 + s, :].astype(bf)
            return 0

        lax.fori_loop(0, PAIRS + 4, second_part, 0)

    pl.run_scoped(fine_work, pltpu.VMEM((36, 80, 640), f32))

    own.wait()

    def got_row(step, _):
        k = lax.rem(c + step, COLS) + 3
        pltpu.make_async_copy(window_row.at[pl.ds(0, 32), :], patch_in.at[k], patch_recv.at[k]).wait()
        return 0

    lax.fori_loop(1, COLS, got_row, 0)
    for k in range(3):
        for cond, slot in ((above, k), (below, 19 + k)):
            @pl.when(cond)
            def _(slot=slot):
                pltpu.make_async_copy(window_row.at[pl.ds(0, 32), :], patch_in.at[slot], patch_recv.at[slot]).wait()

    def coarse_work(grid, cells1, cells2, cells3, keys, turned):
        values = patch_in[...].astype(f32).reshape(22 * 32, 384)
        for t in range(3):
            grid[t] = silu(values[:, 128 * t : 128 * t + 128])
        cells1[520:568, :] = jnp.zeros((48, 384), f32)
        cells2[400:432, :] = jnp.zeros((32, 384), f32)
        cells3[360:384, :] = jnp.zeros((24, 384), f32)
        for t in range(3):
            lanes = slice(128 * t, 128 * t + 128)
            for m in range(22):
                cells1[24 * m : 24 * m + 24, lanes] = jnp.concatenate(
                    [grid[t, pl.ds(m + 1, 22, stride=32), :], jnp.zeros((2, 128), f32)], axis=0)
        for t in range(3):
            grid[t] = values[:, 128 * t : 128 * t + 128]
        for t in range(3):
            lanes = slice(128 * t, 128 * t + 128)
            for m in range(18):
                cells3[PITCH * m : PITCH * m + PITCH, lanes] = grid[t, pl.ds(64 + m + 3, PITCH, stride=32), :]
        for a in range(3):
            for b in range(3):
                k = 3 * a + b
                first = 24 * b + a
                keys[:, 384 * k : 384 * k + 384] = cells1[first : first + 512, :].astype(bf)
        widen = lambda w: jnp.concatenate([w, gap], axis=1)
        first_taps = jnp.concatenate([widen(taps_raw[2, k]) for k in range(9)], axis=1)
        hidden = lax.dot_general(first_taps, keys[:, 0:3456], contract, preferred_element_type=f32)
        hidden = jnp.concatenate([silu(hidden), jnp.zeros((64, 512), f32)], axis=0)
        turned[...] = jnp.transpose(hidden)
        field_row = lax.broadcasted_iota(jnp.int32, (PITCH, 384), 0) + (16 * r - 2)
        row_ok = jnp.logical_and(field_row >= 0, field_row < 128)
        for m in range(20):
            col = 16 * c - 2 + m
            ok = jnp.logical_and(row_ok, jnp.logical_and(col >= 0, col < 256))
            cells2[PITCH * m : PITCH * m + PITCH, :] = jnp.where(ok, turned[24 * m : 24 * m + PITCH, :], 0.0)
        for a in range(3):
            for b in range(3):
                k = 3 * a + b
                first = PITCH * b + a
                keys[0:384, 384 * k : 384 * k + 384] = cells2[first : first + 384, :].astype(bf)
        keys[0:384, 3456:3840] = cells3[...].astype(bf)
        eye = lax.broadcasted_iota(jnp.int32, (C, 384), 0) == lax.broadcasted_iota(jnp.int32, (C, 384), 1)
        second_taps = jnp.concatenate([widen(taps_raw[3, k]) for k in range(9)] + [eye.astype(f32).astype(bf)], axis=1)
        coarse = lift * lax.dot_general(second_taps, keys[0:384, :], contract, preferred_element_type=f32)
        for h in range(2):
            part = coarse if h == 0 else pltpu.roll(coarse, 384 - 160, axis=1)
            part = part[:, 0:256]
            high = part.astype(bf)
            blocks[h, :, 0:256] = high
            blocks[h, :, 256:512] = (part - high.astype(f32)).astype(bf)

    pl.run_scoped(
        coarse_work,
        pltpu.VMEM((3, 704, 128), f32),
        pltpu.VMEM((568, 384), f32),
        pltpu.VMEM((432, 384), f32),
        pltpu.VMEM((384, 384), f32),
        pltpu.VMEM((512, 3840), bf),
        pltpu.VMEM((512, 384), f32),
    )

    writes = {}

    def blend(h, rim, source, slot):
        for old in writes.pop(slot, ()):
            old.wait()
        for u in range(CHUNK // 4):
            block = jnp.transpose(acc[source, :, 128 * u : 128 * u + 128])
            for v in range(4):
                pp = 4 * u + v
                cells = raw[2 + CHUNK * h + pp]
                if rim:
                    cells = jnp.concatenate([cells[0:16], cells[48:64]], axis=0)
                else:
                    cells = cells[16:48]
                staged[slot, :, PAIR * pp : PAIR * (pp + 1)] = (
                    keep * cells.astype(f32) + gain * block[32 * v : 32 * v + 32])
        lanes = pl.ds(PAIR * CHUNK * h, PAIR * CHUNK)
        if rim:
            parts = [(pl.ds(0, 16), pl.ds(0, 16)), (pl.ds(16, 16), pl.ds(48, 16))]
        else:
            parts = [(pl.ds(0, 32), pl.ds(16, 32))]
        writes[slot] = []
        for k, (here, there) in enumerate(parts):
            cp = pltpu.make_async_copy(staged.at[slot, here], out.at[there, lanes], out_sem.at[2 * slot + k])
            cp.start()
            writes[slot].append(cp)

    for h in range(2):
        for par in range(2):
            acc[h, C * par : C * par + C, :] += lax.dot_general(
                blocks[h], shares(h, par, False), contract, preferred_element_type=f32)
        target = 2 if h == 0 else 0
        for par in range(2):
            rhs = jnp.concatenate(keys_of(h, par, True) + [shares(h, par, True)], axis=1)
            lhs = jnp.concatenate([taps[par], blocks[h]], axis=1)
            acc[target, C * par : C * par + C, :] = lax.dot_general(lhs, rhs, contract, preferred_element_type=f32)
        if h == 0:
            blend(0, False, 0, 0)
        else:
            blend(1, False, 1, 1)
            blend(0, True, 2, 0)
            blend(1, True, 0, 1)
    for group_of in writes.values():
        for cp in group_of:
            cp.wait()

    for k in range(8):
        @pl.when(present(*sides[k][0]))
        def _(k=k):
            side_copy(k).wait_send()

    def sent_row(step, _):
        patch_copy(r, lax.rem(c + step, COLS), c + 3, 0).wait_send()
        return 0

    lax.fori_loop(1, COLS, sent_row, 0)

    @pl.when(down)
    def _():
        def one(step, _):
            patch_copy(r + 1, lax.rem(c + step, COLS), c - 13, 1).wait_send()
            return 0
        lax.fori_loop(0, COLS, one, 0)

    @pl.when(up)
    def _():
        def one(step, _):
            patch_copy(r - 1, lax.rem(c + step, COLS), c + 19, 1).wait_send()
            return 0
        lax.fori_loop(0, COLS, one, 0)


def whole(*arrays):
    f32, bf = jnp.float32, jnp.bfloat16
    any_spec = pl.BlockSpec(memory_space=pl.ANY)
    return pl.pallas_call(
        whole_kernel,
        out_shape=jax.ShapeDtypeStruct((64, 20480), f32),
        in_specs=[pl.BlockSpec(memory_space=pltpu.SMEM)] + [any_spec] * 6,
        out_specs=any_spec,
        scratch_shapes=[
            pltpu.VMEM((36, 64, 640), bf),
            pltpu.VMEM((5, 36, 64, 640), bf),
            pltpu.VMEM((4, 9, C, C), bf),
            pltpu.VMEM((2, C, KEYS), bf),
            pltpu.VMEM((2, 8, 16, 640), bf),
            pltpu.VMEM((2, 8, 16, 640), bf),
            pltpu.VMEM((4, 16, 640), bf),
            pltpu.VMEM((4, 16, 640), bf),
            pltpu.VMEM((C, 256), bf),
            pltpu.VMEM((288, 384), bf),
            pltpu.VMEM((22, 32, 384), bf),
            pltpu.VMEM((2, C, 512), bf),
            pltpu.VMEM((3, PAIR, CELLS), f32),
            pltpu.VMEM((2, 32, PAIR * CHUNK), f32),
            pltpu.SemaphoreType.DMA((PAIRS + 1,)),
            pltpu.SemaphoreType.DMA((4,)),
            pltpu.SemaphoreType.DMA((4,)),
            pltpu.SemaphoreType.DMA((8,)),
            pltpu.SemaphoreType.DMA((8,)),
            pltpu.SemaphoreType.DMA((2, COLS)),
            pltpu.SemaphoreType.DMA((22,)),
        ],
        compiler_params=pltpu.CompilerParams(collective_id=0, has_side_effects=True, vmem_limit_bytes=VMEM_LIMIT),
        name="whole",
    )(*arrays)


def on_device(coarse_latent, fine_latent, timestep, coarse_first, coarse_second, local_weight, dilated_weight):
    flat = lambda w: w.reshape(9, C, C)
    return whole(
        timestep, fine_latent, coarse_latent.reshape(C, 256),
        flat(coarse_first), flat(coarse_second), flat(local_weight), flat(dilated_weight))


def solution(mesh):
    placed = (P(None, ("row", "col"), None), P("row", "col"), P(), P(), P(), P(), P())
    return jax.shard_map(
        on_device, mesh=mesh, in_specs=placed, out_specs=P("row", "col"), check_vma=False
    )
```

```python
import functools
import math

import jax
import jax.numpy as jnp
from jax import lax
from jax.experimental import pallas as pl
from jax.experimental.pallas import tpu as pltpu
from jax.sharding import PartitionSpec as P

STEPS = 50
C = 320
ROWS = 8
COLS = 16
PAIR = 2 * C
TALL = 64
PAIRS = 32
CHUNK = 16
CELLS = CHUNK * 32
SHIFTS = (-4, -1, 0, 1, 4)
KEYS = 6144
PITCH = 20
MESH = pl.DeviceIdType.MESH
VMEM_LIMIT = 60 * 1024 * 1024


def silu(x):
    return x / (1.0 + jnp.exp(-x))


def factors(timestep):
    angle = jnp.full((8, 128), timestep[0].astype(jnp.float32) * (math.pi / STEPS), jnp.float32)
    mix = (1.0 + jnp.cos(angle)) * 0.5
    skip = mix * mix * mix
    gain = (1.0 - skip) * mix
    return tuple(v[0:1, 0:1] for v in ((1.0 - mix) / mix, skip / gain, 1.0 - skip, gain))


def tap_pieces(parity):
    out = []
    for s in (1, 2, 3):
        if parity == 0:
            out += [(s, -1, 2, 3), (s, 0, 0, 5)]
        else:
            out += [(s, 0, 0, 5), (s, 1, 0, 3)]
    first = 0 if parity == 0 else 2
    for s in (0, 2, 4):
        for off in (-2, 0, 2):
            if s == 2 and off == 0:
                continue
            out.append((s, off, first, 3))
    return out


def whole_kernel(
    timestep, fine, coarse_row, coarse_first, coarse_second, local_weight, dilated_weight, out,
    raw, shifted, taps_raw, taps, packed, edges, corner_out, corners, row_in, window_row, patch_in, blocks, acc, staged,
    lifted, grid, cells1, cells2, cells3, keys, turned,
    in_sem, w_sem, out_sem, send_sem, recv_sem, patch_send, patch_recv,
):
    f32, bf = jnp.float32, jnp.bfloat16
    r = lax.axis_index("row")
    c = lax.axis_index("col")
    above = r > 0
    below = r < ROWS - 1
    down = jnp.logical_and(below, c >= 13)
    up = jnp.logical_and(above, c < 3)

    def present(dr, dc):
        ok = None
        for cond, need in ((above, dr < 0), (below, dr > 0), (c > 0, dc < 0), (c < COLS - 1, dc > 0)):
            if need:
                ok = cond if ok is None else jnp.logical_and(ok, cond)
        return ok

    barrier = pltpu.get_barrier_semaphore()

    def greet(dev):
        pl.semaphore_signal(barrier, inc=1, device_id=dev, device_id_type=MESH)

    def greet_row(step, _):
        greet((r, lax.rem(c + step, COLS)))
        return 0

    lax.fori_loop(1, COLS, greet_row, 0)
    diagonal = ((-1, -1), (-1, 0), (-1, 1), (1, -1), (1, 0), (1, 1))
    expected = COLS - 1 + jnp.where(down, COLS, 0) + jnp.where(up, COLS, 0)
    for step in diagonal:
        @pl.when(present(*step))
        def _(step=step):
            greet((r + step[0], c + step[1]))
        expected = expected + jnp.where(present(*step), 1, 0)
    for k in range(3):
        @pl.when(above)
        def _(k=k):
            greet((r - 1, 13 + k))

        @pl.when(below)
        def _(k=k):
            greet((r + 1, k))

    row_load = pltpu.make_async_copy(coarse_row, row_in, in_sem.at[PAIRS])
    row_load.start()
    loads = []
    for p in range(PAIRS):
        cp = pltpu.make_async_copy(fine.at[:, pl.ds(PAIR * p, PAIR)], raw.at[p + 2], in_sem.at[p])
        cp.start()
        loads.append(cp)
    w_loads = []
    for k, ref in enumerate((dilated_weight, local_weight, coarse_first, coarse_second)):
        cp = pltpu.make_async_copy(ref, taps_raw.at[k], w_sem.at[k])
        cp.start()
        w_loads.append(cp)

    side_zero = jnp.zeros((2, TALL, PAIR), bf)

    @pl.when(c == 0)
    def _():
        raw[0:2] = side_zero
        corners[0] = jnp.zeros((8, PAIR), bf)
        corners[2] = jnp.zeros((8, PAIR), bf)

    @pl.when(c == COLS - 1)
    def _():
        raw[34:36] = side_zero
        corners[1] = jnp.zeros((8, PAIR), bf)
        corners[3] = jnp.zeros((8, PAIR), bf)

    @pl.when(jnp.logical_not(above))
    def _():
        edges[0] = jnp.zeros((8, 16, PAIR), bf)
        corners[0] = jnp.zeros((8, PAIR), bf)
        corners[1] = jnp.zeros((8, PAIR), bf)
        patch_in[0:3] = jnp.zeros((3, 3, 8, 384), bf)

    @pl.when(jnp.logical_not(below))
    def _():
        edges[1] = jnp.zeros((8, 16, PAIR), bf)
        corners[2] = jnp.zeros((8, PAIR), bf)
        corners[3] = jnp.zeros((8, PAIR), bf)
        patch_in[19:22] = jnp.zeros((3, 3, 8, 384), bf)

    row_load.wait()
    turned_row = jnp.concatenate([row_in[...].astype(f32), jnp.zeros((64, 256), f32)], axis=0)
    window = jnp.concatenate(
        [jnp.zeros((4, 384), f32), jnp.transpose(turned_row), jnp.zeros((12, 384), f32)], axis=0)
    window_row[...] = window.reshape(34, 8, 384).astype(bf)
    for cp in loads:
        cp.wait()
    for slot, base, first in ((0, 0, 0), (1, 48, 12)):
        tops = {}
        for p in range(PAIRS):
            tops[p] = raw[2 + p, base : base + 16, :].astype(f32)[first : first + 4]
        for q in range(8):
            packed[slot, q] = jnp.concatenate([tops[8 * g + q] for g in range(4)], axis=0).astype(bf)
        for k, p in ((0, 30), (1, 0)):
            spot = k if slot == 1 else 2 + k
            corner_out[spot] = jnp.concatenate([tops[p], tops[p + 1]], axis=0).astype(bf)
    pl.semaphore_wait(barrier, expected)

    last = pl.ds(32, 2)
    head = pl.ds(2, 2)
    sides = (
        ((0, 1), raw.at[last], raw.at[pl.ds(0, 2)]),
        ((0, -1), raw.at[head], raw.at[pl.ds(34, 2)]),
        ((1, 0), packed.at[1], edges.at[0]),
        ((-1, 0), packed.at[0], edges.at[1]),
        ((1, 1), corner_out.at[0], corners.at[0]),
        ((1, -1), corner_out.at[1], corners.at[1]),
        ((-1, 1), corner_out.at[2], corners.at[2]),
        ((-1, -1), corner_out.at[3], corners.at[3]),
    )

    def side_copy(k):
        step, src, dst = sides[k]
        return pltpu.make_async_remote_copy(
            src_ref=src, dst_ref=dst, send_sem=send_sem.at[k], recv_sem=recv_sem.at[k],
            device_id=(r + step[0], c + step[1]), device_id_type=MESH)

    for k in range(8):
        @pl.when(present(*sides[k][0]))
        def _(k=k):
            side_copy(k).start()

    def window(target):
        return window_row.at[pl.ds(2 * target, 3)]

    def patch_copy(dev_r, dev_c, k, slot):
        return pltpu.make_async_remote_copy(
            src_ref=window(dev_c), dst_ref=patch_in.at[k], send_sem=patch_send.at[slot, dev_c],
            recv_sem=patch_recv.at[k], device_id=(dev_r, dev_c), device_id_type=MESH)

    ratio, lift, keep, gain = factors(timestep)

    for cp in w_loads:
        cp.wait()
    gap = jnp.zeros((C, 64), bf)
    dilated = lambda a, b: taps_raw[0, 3 * a + b]
    local = lambda a, b: (ratio * taps_raw[1, 3 * a + b].astype(f32)).astype(bf)
    for par in range(2):
        at = 0
        for a in range(3):
            row = []
            for b in range(3):
                if a == 1 and b == 1:
                    row.append((dilated(1, 1).astype(f32) + ratio * taps_raw[1, 4].astype(f32)).astype(bf))
                else:
                    row.append(local(a, b))
            row = [gap] + row if par == 0 else row + [gap]
            taps[par, :, at : at + 1024] = jnp.concatenate(row, axis=1)
            at += 1024
        for a in range(3):
            for b in range(3):
                if a == 1 and b == 1:
                    continue
                w = dilated(a, b)
                taps[par, :, at : at + 384] = jnp.concatenate([w, gap] if par == 0 else [gap, w], axis=1)
                at += 384
    contract = (((1,), (1,)), ((), ()))

    lane = lax.broadcasted_iota(jnp.int32, (TALL, 256), 1)
    group = jnp.zeros((TALL, 256), jnp.int32)
    for t in range(1, 13):
        group = group + (lane >= PITCH * t).astype(jnp.int32)
    lane_row = (lane - PITCH * group + (16 * r - 1)).astype(f32)
    lane_col = (group[0:8] + (16 * c - 1)).astype(f32)
    fine_row = (lax.broadcasted_iota(jnp.int32, (TALL, 256), 0) + 64 * r).astype(f32)
    where_row = jnp.clip((fine_row + 0.5) * 0.25 - 0.5, 0.0, 127.0)
    row_share = jnp.maximum(1.0 - jnp.abs(where_row - lane_row), 0.0)
    base_col = (jnp.zeros((8, 256), jnp.int32) + 64 * c).astype(f32)
    inner = row_share[16:48].reshape(4, 8, 256)
    outer = jnp.concatenate([row_share[0:16], row_share[48:64]], axis=0).reshape(4, 8, 256)

    def shares(h, par, rim):
        out = []
        for pp in range(CHUNK):
            spot = jnp.clip((base_col + (32 * h + 2 * pp + par + 0.5)) * 0.25 - 0.5, 0.0, 255.0)
            col_share = jnp.maximum(1.0 - jnp.abs(spot - (lane_col + 8 * h)), 0.0)
            part = ((outer if rim else inner) * col_share[None]).reshape(32, 256)
            out.append(jnp.concatenate([part, part], axis=1).astype(bf))
        return jnp.concatenate(out, axis=0)

    def keys_of(h, par, rim):
        pieces = []
        for s, off, tile, n in tap_pieces(par):
            cells = pl.ds(2 + CHUNK * h + off, CHUNK)
            lanes = slice(128 * tile, 128 * (tile + n))
            if rim:
                part = jnp.concatenate([shifted[s, cells, 0:16, lanes], shifted[s, cells, 48:64, lanes]], axis=1)
            else:
                part = shifted[s, cells, 16:48, lanes]
            pieces.append(part.reshape(CELLS, 128 * n))
        return pieces

    def arrived(k):
        step = sides[k][0]

        @pl.when(present(-step[0], -step[1]))
        def _():
            side_copy(k).wait_recv()

    def first_part(p, _):
        values = silu(raw[p].astype(f32))
        lifted[p, 8:72, :] = values
        shifted[2, p] = values.astype(bf)
        for k in (0, 1, 3, 4):
            s = SHIFTS[k]
            shifted[k, p, 16:48, :] = lifted[p, 24 + s : 56 + s, :].astype(bf)
        return 0

    def second_part(p):
        for k in (0, 1, 3, 4):
            s = SHIFTS[k]
            shifted[k, p, 0:16, :] = lifted[p, 8 + s : 24 + s, :].astype(bf)
            shifted[k, p, 48:64, :] = lifted[p, 56 + s : 72 + s, :].astype(bf)

    def convolve(h, par, rim, lifts=False):
        pieces = keys_of(h, par, rim)
        lhs = taps[par]
        if lifts:
            pieces = pieces + [shares(h, par, rim)]
            lhs = jnp.concatenate([lhs, blocks[h]], axis=1)
        acc[2 * h + rim, C * par : C * par + C, :] = lax.dot_general(
            lhs, jnp.concatenate(pieces, axis=1), contract, preferred_element_type=f32)

    def raise_by(h, par, rim):
        acc[2 * h + rim, C * par : C * par + C, :] += lax.dot_general(
            blocks[h], shares(h, par, rim), contract, preferred_element_type=f32)

    lax.fori_loop(2, 20, first_part, 0)

    own = pltpu.make_async_copy(window(c), patch_in.at[c + 3], patch_recv.at[c + 3])
    own.start()

    def send_row(step, _):
        patch_copy(r, lax.rem(c + step, COLS), c + 3, 0).start()
        return 0

    lax.fori_loop(1, COLS, send_row, 0)

    @pl.when(down)
    def _():
        def one(step, _):
            patch_copy(r + 1, lax.rem(c + step, COLS), c - 13, 1).start()
            return 0
        lax.fori_loop(0, COLS, one, 0)

    @pl.when(up)
    def _():
        def one(step, _):
            patch_copy(r - 1, lax.rem(c + step, COLS), c + 19, 1).start()
            return 0
        lax.fori_loop(0, COLS, one, 0)

    arrived(0)
    arrived(1)
    first_part(0, 0)
    first_part(1, 0)
    convolve(0, 0, False)
    for p in range(20, 28):
        first_part(p, 0)
    convolve(0, 1, False)
    for p in range(28, 36):
        first_part(p, 0)
    convolve(1, 0, False)
    convolve(1, 1, False)
    for k in range(2, 8):
        arrived(k)
    for slot, base in ((0, 4), (1, 72)):
        for q in range(8):
            block = silu(edges[slot, q].astype(f32))
            for g in range(4):
                lifted[2 + 8 * g + q, base : base + 4, :] = block[4 * g : 4 * g + 4]
        for k, first in ((0, 0), (1, 34)):
            block = silu(corners[2 * slot + k].astype(f32))
            for p in range(2):
                lifted[first + p, base : base + 4, :] = block[4 * p : 4 * p + 4]
    for p in range(20):
        second_part(p)
    convolve(0, 0, True)
    for p in range(20, 36):
        second_part(p)

    own.wait()

    def got_row(step, _):
        k = lax.rem(c + step, COLS) + 3
        pltpu.make_async_copy(window_row.at[pl.ds(0, 3)], patch_in.at[k], patch_recv.at[k]).wait()
        return 0

    lax.fori_loop(1, COLS, got_row, 0)
    for k in range(3):
        for cond, slot in ((above, k), (below, 19 + k)):
            @pl.when(cond)
            def _(slot=slot):
                pltpu.make_async_copy(window_row.at[pl.ds(0, 3)], patch_in.at[slot], patch_recv.at[slot]).wait()

    values = patch_in[...].astype(f32).reshape(22 * 24, 384)
    for t in range(3):
        grid[t] = silu(values[:, 128 * t : 128 * t + 128])
    cells1[520:568, :] = jnp.zeros((48, 384), f32)
    cells2[400:432, :] = jnp.zeros((32, 384), f32)
    cells3[360:384, :] = jnp.zeros((24, 384), f32)
    for t in range(3):
        lanes = slice(128 * t, 128 * t + 128)
        for m in range(22):
            cells1[24 * m : 24 * m + 24, lanes] = jnp.concatenate(
                [grid[t, pl.ds(m + 1, 22, stride=24), :], jnp.zeros((2, 128), f32)], axis=0)
    for t in range(3):
        grid[t] = values[:, 128 * t : 128 * t + 128]
    for t in range(3):
        lanes = slice(128 * t, 128 * t + 128)
        for m in range(18):
            cells3[PITCH * m : PITCH * m + PITCH, lanes] = grid[t, pl.ds(48 + m + 3, PITCH, stride=24), :]
    for a in range(3):
        for b in range(3):
            k = 3 * a + b
            first = 24 * b + a
            keys[:, 384 * k : 384 * k + 384] = cells1[first : first + 512, :].astype(bf)
    convolve(0, 1, True)
    widen = lambda w: jnp.concatenate([w, gap], axis=1)
    first_taps = jnp.concatenate([widen(taps_raw[2, k]) for k in range(9)], axis=1)
    hidden = lax.dot_general(first_taps, keys[:, 0:3456], contract, preferred_element_type=f32)
    hidden = jnp.concatenate([silu(hidden), jnp.zeros((64, 512), f32)], axis=0)
    turned[...] = jnp.transpose(hidden)
    field_row = lax.broadcasted_iota(jnp.int32, (PITCH, 384), 0) + (16 * r - 2)
    row_ok = jnp.logical_and(field_row >= 0, field_row < 128)
    for m in range(20):
        col = 16 * c - 2 + m
        ok = jnp.logical_and(row_ok, jnp.logical_and(col >= 0, col < 256))
        cells2[PITCH * m : PITCH * m + PITCH, :] = jnp.where(ok, turned[24 * m : 24 * m + PITCH, :], 0.0)
    for a in range(3):
        for b in range(3):
            k = 3 * a + b
            first = PITCH * b + a
            keys[0:384, 384 * k : 384 * k + 384] = cells2[first : first + 384, :].astype(bf)
    keys[0:384, 3456:3840] = cells3[...].astype(bf)
    eye = lax.broadcasted_iota(jnp.int32, (C, 384), 0) == lax.broadcasted_iota(jnp.int32, (C, 384), 1)
    second_taps = jnp.concatenate([widen(taps_raw[3, k]) for k in range(9)] + [eye.astype(f32).astype(bf)], axis=1)
    coarse = lift * lax.dot_general(second_taps, keys[0:384, :], contract, preferred_element_type=f32)
    for h in range(2):
        part = coarse if h == 0 else pltpu.roll(coarse, 384 - 160, axis=1)
        part = part[:, 0:256]
        high = part.astype(bf)
        blocks[h, :, 0:256] = high
        blocks[h, :, 256:512] = (part - high.astype(f32)).astype(bf)
    writes = {}

    def blend(h, rim, source, slot):
        for old in writes.pop(slot, ()):
            old.wait()
        for u in range(CHUNK // 4):
            block = jnp.transpose(acc[source, :, 128 * u : 128 * u + 128])
            for v in range(4):
                pp = 4 * u + v
                cells = raw[2 + CHUNK * h + pp]
                if rim:
                    cells = jnp.concatenate([cells[0:16], cells[48:64]], axis=0)
                else:
                    cells = cells[16:48]
                staged[slot, :, PAIR * pp : PAIR * (pp + 1)] = (
                    keep * cells.astype(f32) + gain * block[32 * v : 32 * v + 32])
        lanes = pl.ds(PAIR * CHUNK * h, PAIR * CHUNK)
        if rim:
            parts = [(pl.ds(0, 16), pl.ds(0, 16)), (pl.ds(16, 16), pl.ds(48, 16))]
        else:
            parts = [(pl.ds(0, 32), pl.ds(16, 32))]
        writes[slot] = []
        for k, (here, there) in enumerate(parts):
            cp = pltpu.make_async_copy(staged.at[slot, here], out.at[there, lanes], out_sem.at[2 * slot + k])
            cp.start()
            writes[slot].append(cp)

    def raised(h, rim):
        for par in range(2):
            raise_by(h, par, rim)

    raised(0, False)
    raised(0, True)
    blend(0, False, 0, 0)
    convolve(1, 0, True, True)
    blend(0, True, 1, 1)
    raised(1, False)
    blend(1, False, 2, 0)
    convolve(1, 1, True, True)
    blend(1, True, 3, 1)
    for group_of in writes.values():
        for cp in group_of:
            cp.wait()

    for k in range(8):
        @pl.when(present(*sides[k][0]))
        def _(k=k):
            side_copy(k).wait_send()

    def sent_row(step, _):
        patch_copy(r, lax.rem(c + step, COLS), c + 3, 0).wait_send()
        return 0

    lax.fori_loop(1, COLS, sent_row, 0)

    @pl.when(down)
    def _():
        def one(step, _):
            patch_copy(r + 1, lax.rem(c + step, COLS), c - 13, 1).wait_send()
            return 0
        lax.fori_loop(0, COLS, one, 0)

    @pl.when(up)
    def _():
        def one(step, _):
            patch_copy(r - 1, lax.rem(c + step, COLS), c + 19, 1).wait_send()
            return 0
        lax.fori_loop(0, COLS, one, 0)


def whole(*arrays):
    f32, bf = jnp.float32, jnp.bfloat16
    any_spec = pl.BlockSpec(memory_space=pl.ANY)
    return pl.pallas_call(
        whole_kernel,
        out_shape=jax.ShapeDtypeStruct((64, 20480), f32),
        in_specs=[pl.BlockSpec(memory_space=pltpu.SMEM)] + [any_spec] * 6,
        out_specs=any_spec,
        scratch_shapes=[
            pltpu.VMEM((36, 64, 640), bf),
            pltpu.VMEM((5, 36, 64, 640), bf),
            pltpu.VMEM((4, 9, C, C), bf),
            pltpu.VMEM((2, C, KEYS), bf),
            pltpu.VMEM((2, 8, 16, 640), bf),
            pltpu.VMEM((2, 8, 16, 640), bf),
            pltpu.VMEM((4, 8, 640), bf),
            pltpu.VMEM((4, 8, 640), bf),
            pltpu.VMEM((C, 256), bf),
            pltpu.VMEM((34, 8, 384), bf),
            pltpu.VMEM((22, 3, 8, 384), bf),
            pltpu.VMEM((2, C, 512), bf),
            pltpu.VMEM((4, PAIR, CELLS), f32),
            pltpu.VMEM((2, 32, PAIR * CHUNK), f32),
            pltpu.VMEM((36, 80, 640), f32),
            pltpu.VMEM((3, 528, 128), f32),
            pltpu.VMEM((568, 384), f32),
            pltpu.VMEM((432, 384), f32),
            pltpu.VMEM((384, 384), f32),
            pltpu.VMEM((512, 3840), bf),
            pltpu.VMEM((512, 384), f32),
            pltpu.SemaphoreType.DMA((PAIRS + 1,)),
            pltpu.SemaphoreType.DMA((4,)),
            pltpu.SemaphoreType.DMA((4,)),
            pltpu.SemaphoreType.DMA((8,)),
            pltpu.SemaphoreType.DMA((8,)),
            pltpu.SemaphoreType.DMA((2, COLS)),
            pltpu.SemaphoreType.DMA((22,)),
        ],
        compiler_params=pltpu.CompilerParams(collective_id=0, has_side_effects=True, vmem_limit_bytes=VMEM_LIMIT),
        name="whole",
    )(*arrays)


def on_device(coarse_latent, fine_latent, timestep, coarse_first, coarse_second, local_weight, dilated_weight):
    flat = lambda w: w.reshape(9, C, C)
    return whole(
        timestep, fine_latent, coarse_latent.reshape(C, 256),
        flat(coarse_first), flat(coarse_second), flat(local_weight), flat(dilated_weight))


def solution(mesh):
    placed = (P(None, ("row", "col"), None), P("row", "col"), P(), P(), P(), P(), P())
    return jax.shard_map(
        on_device, mesh=mesh, in_specs=placed, out_specs=P("row", "col"), check_vma=False
    )
```

```python
import functools
import math

import jax
import jax.numpy as jnp
from jax import lax
from jax.experimental import pallas as pl
from jax.experimental.pallas import tpu as pltpu
from jax.sharding import PartitionSpec as P

STEPS = 50
C = 320
ROWS = 8
COLS = 16
PAIR = 2 * C
TALL = 64
PAIRS = 32
CHUNK = 16
CELLS = CHUNK * 32
SHIFTS = (-4, -1, 0, 1, 4)
KEYS = 6144
PITCH = 20
MESH = pl.DeviceIdType.MESH
VMEM_LIMIT = 60 * 1024 * 1024


def silu(x):
    half = 0.5 * x
    return half + half * jnp.tanh(half)


def factors(timestep):
    angle = jnp.full((8, 128), timestep[0].astype(jnp.float32) * (math.pi / STEPS), jnp.float32)
    mix = (1.0 + jnp.cos(angle)) * 0.5
    skip = mix * mix * mix
    gain = (1.0 - skip) * mix
    return tuple(v[0:1, 0:1] for v in ((1.0 - mix) / mix, skip / gain, 1.0 - skip, gain))


def tap_pieces(parity):
    out = []
    for s in (1, 2, 3):
        if parity == 0:
            out += [(s, -1, 2, 3), (s, 0, 0, 5)]
        else:
            out += [(s, 0, 0, 5), (s, 1, 0, 3)]
    first = 0 if parity == 0 else 2
    for s in (0, 2, 4):
        for off in (-2, 0, 2):
            if s == 2 and off == 0:
                continue
            out.append((s, off, first, 3))
    return out


def whole_kernel(
    timestep, fine, coarse_row, coarse_first, coarse_second, local_weight, dilated_weight, out,
    raw, shifted, taps_raw, taps, packed, edges, corner_out, corners, row_in, window_row, patch_in, blocks, acc, staged,
    lifted, grid, cells1, cells2, cells3, keys, turned,
    in_sem, w_sem, out_sem, send_sem, recv_sem, patch_send, patch_recv, pass_send, pass_recv,
):
    f32, bf = jnp.float32, jnp.bfloat16
    r = lax.axis_index("row")
    c = lax.axis_index("col")
    above = r > 0
    below = r < ROWS - 1

    def present(dr, dc):
        ok = None
        for cond, need in ((above, dr < 0), (below, dr > 0), (c > 0, dc < 0), (c < COLS - 1, dc > 0)):
            if need:
                ok = cond if ok is None else jnp.logical_and(ok, cond)
        return ok

    row_load = pltpu.make_async_copy(coarse_row, row_in, in_sem.at[PAIRS])
    row_load.start()
    loads = []
    for p in range(PAIRS):
        cp = pltpu.make_async_copy(fine.at[:, pl.ds(PAIR * p, PAIR)], raw.at[p + 2], in_sem.at[p])
        cp.start()
        loads.append(cp)

    barrier = pltpu.get_barrier_semaphore()

    def greet(dev):
        pl.semaphore_signal(barrier, inc=1, device_id=dev, device_id_type=MESH)

    def greet_row(step, _):
        greet((r, lax.rem(c + step, COLS)))
        return 0

    lax.fori_loop(1, COLS, greet_row, 0)
    diagonal = ((-1, -1), (-1, 0), (-1, 1), (1, -1), (1, 0), (1, 1))
    expected = jnp.int32(COLS - 1)
    for step in diagonal:
        @pl.when(present(*step))
        def _(step=step):
            greet((r + step[0], c + step[1]))
        expected = expected + jnp.where(present(*step), 1, 0)
    side_zero = jnp.zeros((2, TALL, PAIR), bf)

    @pl.when(c == 0)
    def _():
        raw[0:2] = side_zero
        corners[0] = jnp.zeros((8, PAIR), bf)
        corners[2] = jnp.zeros((8, PAIR), bf)

    @pl.when(c == COLS - 1)
    def _():
        raw[34:36] = side_zero
        corners[1] = jnp.zeros((8, PAIR), bf)
        corners[3] = jnp.zeros((8, PAIR), bf)

    @pl.when(jnp.logical_not(above))
    def _():
        edges[0] = jnp.zeros((8, 16, PAIR), bf)
        corners[0] = jnp.zeros((8, PAIR), bf)
        corners[1] = jnp.zeros((8, PAIR), bf)
        patch_in[0:3] = jnp.zeros((3, 3, 8, 384), bf)

    @pl.when(jnp.logical_not(below))
    def _():
        edges[1] = jnp.zeros((8, 16, PAIR), bf)
        corners[2] = jnp.zeros((8, PAIR), bf)
        corners[3] = jnp.zeros((8, PAIR), bf)
        patch_in[19:22] = jnp.zeros((3, 3, 8, 384), bf)

    for cp in loads:
        cp.wait()
    w_loads = []
    for k, ref in enumerate((dilated_weight, local_weight, coarse_first, coarse_second)):
        cp = pltpu.make_async_copy(ref, taps_raw.at[k], w_sem.at[k])
        cp.start()
        w_loads.append(cp)
    for slot, base, first in ((0, 0, 0), (1, 48, 12)):
        tops = {}
        for p in range(PAIRS):
            tops[p] = raw[2 + p, base : base + 16, :].astype(f32)[first : first + 4]
        for q in range(8):
            packed[slot, q] = jnp.concatenate([tops[8 * g + q] for g in range(4)], axis=0).astype(bf)
        for k, p in ((0, 30), (1, 0)):
            spot = k if slot == 1 else 2 + k
            corner_out[spot] = jnp.concatenate([tops[p], tops[p + 1]], axis=0).astype(bf)
    pl.semaphore_wait(barrier, expected)

    last = pl.ds(32, 2)
    head = pl.ds(2, 2)
    sides = (
        ((0, 1), raw.at[last], raw.at[pl.ds(0, 2)]),
        ((0, -1), raw.at[head], raw.at[pl.ds(34, 2)]),
        ((1, 0), packed.at[1], edges.at[0]),
        ((-1, 0), packed.at[0], edges.at[1]),
        ((1, 1), corner_out.at[0], corners.at[0]),
        ((1, -1), corner_out.at[1], corners.at[1]),
        ((-1, 1), corner_out.at[2], corners.at[2]),
        ((-1, -1), corner_out.at[3], corners.at[3]),
    )

    def side_copy(k):
        step, src, dst = sides[k]
        return pltpu.make_async_remote_copy(
            src_ref=src, dst_ref=dst, send_sem=send_sem.at[k], recv_sem=recv_sem.at[k],
            device_id=(r + step[0], c + step[1]), device_id_type=MESH)

    for k in range(8):
        @pl.when(present(*sides[k][0]))
        def _(k=k):
            side_copy(k).start()

    def window(target):
        return window_row.at[pl.ds(2 * target, 3)]

    def patch_copy(dev_c):
        return pltpu.make_async_remote_copy(
            src_ref=window(dev_c), dst_ref=patch_in.at[c + 3], send_sem=patch_send.at[dev_c],
            recv_sem=patch_recv.at[c + 3], device_id=(r, dev_c), device_id_type=MESH)

    row_load.wait()
    turned_row = jnp.concatenate([row_in[...].astype(f32), jnp.zeros((64, 256), f32)], axis=0)
    wide_row = jnp.concatenate(
        [jnp.zeros((4, 384), f32), jnp.transpose(turned_row), jnp.zeros((12, 384), f32)], axis=0)
    window_row[...] = wide_row.reshape(34, 8, 384).astype(bf)
    ratio, lift, keep, gain = factors(timestep)

    for cp in w_loads:
        cp.wait()
    gap = jnp.zeros((C, 64), bf)
    dilated = lambda a, b: taps_raw[0, 3 * a + b]
    local = lambda a, b: (ratio * taps_raw[1, 3 * a + b].astype(f32)).astype(bf)
    def fill_taps(par):
        at = 0
        for a in range(3):
            row = []
            for b in range(3):
                if a == 1 and b == 1:
                    row.append((dilated(1, 1).astype(f32) + ratio * taps_raw[1, 4].astype(f32)).astype(bf))
                else:
                    row.append(local(a, b))
            row = [gap] + row if par == 0 else row + [gap]
            taps[par, :, at : at + 1024] = jnp.concatenate(row, axis=1)
            at += 1024
        for a in range(3):
            for b in range(3):
                if a == 1 and b == 1:
                    continue
                w = dilated(a, b)
                taps[par, :, at : at + 384] = jnp.concatenate([w, gap] if par == 0 else [gap, w], axis=1)
                at += 384

    fill_taps(0)

    contract = (((1,), (1,)), ((), ()))

    lane = lax.broadcasted_iota(jnp.int32, (TALL, 256), 1)
    group = jnp.zeros((TALL, 256), jnp.int32)
    for t in range(1, 13):
        group = group + (lane >= PITCH * t).astype(jnp.int32)
    lane_row = (lane - PITCH * group + (16 * r - 1)).astype(f32)
    lane_col = (group[0:8] + (16 * c - 1)).astype(f32)
    fine_row = (lax.broadcasted_iota(jnp.int32, (TALL, 256), 0) + 64 * r).astype(f32)
    where_row = jnp.clip((fine_row + 0.5) * 0.25 - 0.5, 0.0, 127.0)
    row_share = jnp.maximum(1.0 - jnp.abs(where_row - lane_row), 0.0)
    base_col = (jnp.zeros((8, 256), jnp.int32) + 64 * c).astype(f32)
    inner = row_share[16:48].reshape(4, 8, 256)
    outer = jnp.concatenate([row_share[0:16], row_share[48:64]], axis=0).reshape(4, 8, 256)

    def shares(h, par, rim):
        out = []
        for pp in range(CHUNK):
            spot = jnp.clip((base_col + (32 * h + 2 * pp + par + 0.5)) * 0.25 - 0.5, 0.0, 255.0)
            col_share = jnp.maximum(1.0 - jnp.abs(spot - (lane_col + 8 * h)), 0.0)
            part = ((outer if rim else inner) * col_share[None]).reshape(32, 256)
            out.append(jnp.concatenate([part, part], axis=1).astype(bf))
        return jnp.concatenate(out, axis=0)

    def keys_of(h, par, rim):
        pieces = []
        for s, off, tile, n in tap_pieces(par):
            cells = pl.ds(2 + CHUNK * h + off, CHUNK)
            lanes = slice(128 * tile, 128 * (tile + n))
            if rim:
                part = jnp.concatenate([shifted[s, cells, 0:16, lanes], shifted[s, cells, 48:64, lanes]], axis=1)
            else:
                part = shifted[s, cells, 16:48, lanes]
            pieces.append(part.reshape(CELLS, 128 * n))
        return pieces

    def arrived(k):
        step = sides[k][0]

        @pl.when(present(-step[0], -step[1]))
        def _():
            side_copy(k).wait_recv()

    def first_part(p, _):
        values = silu(raw[p].astype(f32))
        lifted[p, 8:72, :] = values
        shifted[2, p] = values.astype(bf)
        for k in (0, 1, 3, 4):
            s = SHIFTS[k]
            shifted[k, p, 16:48, :] = lifted[p, 24 + s : 56 + s, :].astype(bf)
        return 0

    def second_part(p):
        for k in (0, 1, 3, 4):
            s = SHIFTS[k]
            shifted[k, p, 0:16, :] = lifted[p, 8 + s : 24 + s, :].astype(bf)
            shifted[k, p, 48:64, :] = lifted[p, 56 + s : 72 + s, :].astype(bf)

    def convolve(h, par, rim, lifts=False):
        pieces = keys_of(h, par, rim)
        lhs = taps[par]
        if lifts:
            pieces = pieces + [shares(h, par, rim)]
            lhs = jnp.concatenate([lhs, blocks[h]], axis=1)
        acc[2 * h + rim, C * par : C * par + C, :] = lax.dot_general(
            lhs, jnp.concatenate(pieces, axis=1), contract, preferred_element_type=f32)

    def raise_by(h, par, rim):
        acc[2 * h + rim, C * par : C * par + C, :] += lax.dot_general(
            blocks[h], shares(h, par, rim), contract, preferred_element_type=f32)

    lax.fori_loop(2, 20, first_part, 0)

    own = pltpu.make_async_copy(window(c), patch_in.at[c + 3], patch_recv.at[c + 3])
    own.start()

    def send_row(step, _):
        patch_copy(lax.rem(c + step, COLS)).start()
        return 0

    lax.fori_loop(1, COLS, send_row, 0)
    passes = (
        (below, 1, patch_in.at[pl.ds(16, 3)], patch_in.at[pl.ds(0, 3)]),
        (above, -1, patch_in.at[pl.ds(3, 3)], patch_in.at[pl.ds(19, 3)]),
    )

    def pass_copy(k):
        cond, step, src, dst = passes[k]
        return pltpu.make_async_remote_copy(
            src_ref=src, dst_ref=dst, send_sem=pass_send.at[k], recv_sem=pass_recv.at[k],
            device_id=(r + step, c), device_id_type=MESH)

    arrived(0)
    arrived(1)
    first_part(0, 0)
    first_part(1, 0)
    convolve(0, 0, False)
    fill_taps(1)
    for p in range(20, 28):
        first_part(p, 0)
    convolve(0, 1, False)
    for p in range(28, 36):
        first_part(p, 0)
    convolve(1, 0, False)
    own.wait()

    def got_row(step, _):
        k = lax.rem(c + step, COLS) + 3
        pltpu.make_async_copy(window_row.at[pl.ds(0, 3)], patch_in.at[k], patch_recv.at[k]).wait()
        return 0

    lax.fori_loop(1, COLS, got_row, 0)
    for k in range(2):
        @pl.when(passes[k][0])
        def _(k=k):
            pass_copy(k).start()

    convolve(1, 1, False)
    for k in range(2, 8):
        arrived(k)
    for slot, base in ((0, 4), (1, 72)):
        for q in range(8):
            block = silu(edges[slot, q].astype(f32))
            for g in range(4):
                lifted[2 + 8 * g + q, base : base + 4, :] = block[4 * g : 4 * g + 4]
        for k, first in ((0, 0), (1, 34)):
            block = silu(corners[2 * slot + k].astype(f32))
            for p in range(2):
                lifted[first + p, base : base + 4, :] = block[4 * p : 4 * p + 4]
    for p in range(20):
        second_part(p)
    convolve(0, 0, True)
    for p in range(20, 36):
        second_part(p)

    for k, cond in ((0, above), (1, below)):
        @pl.when(cond)
        def _(k=k):
            pass_copy(k).wait_recv()

    values = patch_in[...].astype(f32).reshape(22 * 24, 384)
    for t in range(3):
        grid[t] = silu(values[:, 128 * t : 128 * t + 128])
    cells1[520:568, :] = jnp.zeros((48, 384), f32)
    cells2[400:432, :] = jnp.zeros((32, 384), f32)
    cells3[360:384, :] = jnp.zeros((24, 384), f32)
    for t in range(3):
        lanes = slice(128 * t, 128 * t + 128)
        for m in range(22):
            cells1[24 * m : 24 * m + 24, lanes] = jnp.concatenate(
                [grid[t, pl.ds(m + 1, 22, stride=24), :], jnp.zeros((2, 128), f32)], axis=0)
    for t in range(3):
        grid[t] = values[:, 128 * t : 128 * t + 128]
    for t in range(3):
        lanes = slice(128 * t, 128 * t + 128)
        for m in range(18):
            cells3[PITCH * m : PITCH * m + PITCH, lanes] = grid[t, pl.ds(48 + m + 3, PITCH, stride=24), :]
    for a in range(3):
        for b in range(3):
            k = 3 * a + b
            first = 24 * b + a
            keys[:, 384 * k : 384 * k + 384] = cells1[first : first + 512, :].astype(bf)
    convolve(0, 1, True)
    widen = lambda w: jnp.concatenate([w, gap], axis=1)
    first_taps = jnp.concatenate([widen(taps_raw[2, k]) for k in range(9)], axis=1)
    hidden = lax.dot_general(first_taps, keys[:, 0:3456], contract, preferred_element_type=f32)
    hidden = jnp.concatenate([silu(hidden), jnp.zeros((64, 512), f32)], axis=0)
    turned[...] = jnp.transpose(hidden)
    field_row = lax.broadcasted_iota(jnp.int32, (PITCH, 384), 0) + (16 * r - 2)
    row_ok = jnp.logical_and(field_row >= 0, field_row < 128)
    for m in range(20):
        col = 16 * c - 2 + m
        ok = jnp.logical_and(row_ok, jnp.logical_and(col >= 0, col < 256))
        cells2[PITCH * m : PITCH * m + PITCH, :] = jnp.where(ok, turned[24 * m : 24 * m + PITCH, :], 0.0)
    for a in range(3):
        for b in range(3):
            k = 3 * a + b
            first = PITCH * b + a
            keys[0:384, 384 * k : 384 * k + 384] = cells2[first : first + 384, :].astype(bf)
    keys[0:384, 3456:3840] = cells3[...].astype(bf)
    eye = lax.broadcasted_iota(jnp.int32, (C, 384), 0) == lax.broadcasted_iota(jnp.int32, (C, 384), 1)
    second_taps = jnp.concatenate([widen(taps_raw[3, k]) for k in range(9)] + [eye.astype(f32).astype(bf)], axis=1)
    coarse = lift * lax.dot_general(second_taps, keys[0:384, :], contract, preferred_element_type=f32)
    for h in range(2):
        part = coarse if h == 0 else pltpu.roll(coarse, 384 - 160, axis=1)
        part = part[:, 0:256]
        high = part.astype(bf)
        blocks[h, :, 0:256] = high
        blocks[h, :, 256:512] = (part - high.astype(f32)).astype(bf)
    writes = {}

    def blend(h, rim, source, slot):
        for old in writes.pop(slot, ()):
            old.wait()
        for u in range(CHUNK // 4):
            block = jnp.transpose(acc[source, :, 128 * u : 128 * u + 128])
            for v in range(4):
                pp = 4 * u + v
                cells = raw[2 + CHUNK * h + pp]
                if rim:
                    cells = jnp.concatenate([cells[0:16], cells[48:64]], axis=0)
                else:
                    cells = cells[16:48]
                staged[slot, :, PAIR * pp : PAIR * (pp + 1)] = (
                    keep * cells.astype(f32) + gain * block[32 * v : 32 * v + 32])
        lanes = pl.ds(PAIR * CHUNK * h, PAIR * CHUNK)
        if rim:
            parts = [(pl.ds(0, 16), pl.ds(0, 16)), (pl.ds(16, 16), pl.ds(48, 16))]
        else:
            parts = [(pl.ds(0, 32), pl.ds(16, 32))]
        writes[slot] = []
        for k, (here, there) in enumerate(parts):
            cp = pltpu.make_async_copy(staged.at[slot, here], out.at[there, lanes], out_sem.at[2 * slot + k])
            cp.start()
            writes[slot].append(cp)

    def raised(h, rim):
        for par in range(2):
            raise_by(h, par, rim)

    raised(0, False)
    raised(0, True)
    blend(0, False, 0, 0)
    convolve(1, 0, True, True)
    blend(0, True, 1, 1)
    raised(1, False)
    blend(1, False, 2, 0)
    convolve(1, 1, True, True)
    blend(1, True, 3, 1)
    for group_of in writes.values():
        for cp in group_of:
            cp.wait()

    for k in range(8):
        @pl.when(present(*sides[k][0]))
        def _(k=k):
            side_copy(k).wait_send()

    def sent_row(step, _):
        patch_copy(lax.rem(c + step, COLS)).wait_send()
        return 0

    lax.fori_loop(1, COLS, sent_row, 0)
    for k in range(2):
        @pl.when(passes[k][0])
        def _(k=k):
            pass_copy(k).wait_send()


def whole(*arrays):
    f32, bf = jnp.float32, jnp.bfloat16
    any_spec = pl.BlockSpec(memory_space=pl.ANY)
    return pl.pallas_call(
        whole_kernel,
        out_shape=jax.ShapeDtypeStruct((64, 20480), f32),
        in_specs=[pl.BlockSpec(memory_space=pltpu.SMEM)] + [any_spec] * 6,
        out_specs=any_spec,
        scratch_shapes=[
            pltpu.VMEM((36, 64, 640), bf),
            pltpu.VMEM((5, 36, 64, 640), bf),
            pltpu.VMEM((4, 9, C, C), bf),
            pltpu.VMEM((2, C, KEYS), bf),
            pltpu.VMEM((2, 8, 16, 640), bf),
            pltpu.VMEM((2, 8, 16, 640), bf),
            pltpu.VMEM((4, 8, 640), bf),
            pltpu.VMEM((4, 8, 640), bf),
            pltpu.VMEM((C, 256), bf),
            pltpu.VMEM((34, 8, 384), bf),
            pltpu.VMEM((22, 3, 8, 384), bf),
            pltpu.VMEM((2, C, 512), bf),
            pltpu.VMEM((4, PAIR, CELLS), f32),
            pltpu.VMEM((2, 32, PAIR * CHUNK), f32),
            pltpu.VMEM((36, 80, 640), f32),
            pltpu.VMEM((3, 528, 128), f32),
            pltpu.VMEM((568, 384), f32),
            pltpu.VMEM((432, 384), f32),
            pltpu.VMEM((384, 384), f32),
            pltpu.VMEM((512, 3840), bf),
            pltpu.VMEM((512, 384), f32),
            pltpu.SemaphoreType.DMA((PAIRS + 1,)),
            pltpu.SemaphoreType.DMA((4,)),
            pltpu.SemaphoreType.DMA((4,)),
            pltpu.SemaphoreType.DMA((8,)),
            pltpu.SemaphoreType.DMA((8,)),
            pltpu.SemaphoreType.DMA((COLS,)),
            pltpu.SemaphoreType.DMA((22,)),
            pltpu.SemaphoreType.DMA((2,)),
            pltpu.SemaphoreType.DMA((2,)),
        ],
        compiler_params=pltpu.CompilerParams(collective_id=0, has_side_effects=True, vmem_limit_bytes=VMEM_LIMIT),
        name="whole",
    )(*arrays)


def store_kernel(held, out, block, in_sem, out_sem):
    lanes = [pl.ds(1280 * k, 1280) for k in range(16)]
    reads = [pltpu.make_async_copy(held.at[:, lanes[k]], block.at[k], in_sem.at[k]) for k in range(16)]
    writes = [pltpu.make_async_copy(block.at[k], out.at[:, lanes[k]], out_sem.at[k]) for k in range(16)]
    for cp in reads:
        cp.start()
    for k in range(16):
        reads[k].wait()
        writes[k].start()
    for cp in writes:
        cp.wait()


def store(held):
    any_spec = pl.BlockSpec(memory_space=pl.ANY)
    return pl.pallas_call(
        store_kernel,
        out_shape=jax.ShapeDtypeStruct((64, 20480), jnp.float32),
        in_specs=[any_spec],
        out_specs=any_spec,
        scratch_shapes=[
            pltpu.VMEM((16, 64, 1280), jnp.float32),
            pltpu.SemaphoreType.DMA((16,)),
            pltpu.SemaphoreType.DMA((16,)),
        ],
        compiler_params=pltpu.CompilerParams(vmem_limit_bytes=VMEM_LIMIT),
        name="store",
    )(held)


def on_device(coarse_latent, fine_latent, timestep, coarse_first, coarse_second, local_weight, dilated_weight):
    flat = lambda w: w.reshape(9, C, C)
    held = whole(
        timestep, fine_latent, coarse_latent.reshape(C, 256),
        flat(coarse_first), flat(coarse_second), flat(local_weight), flat(dilated_weight))
    return store(held)


def solution(mesh):
    placed = (P(None, ("row", "col"), None), P("row", "col"), P(), P(), P(), P(), P())
    return jax.shard_map(
        on_device, mesh=mesh, in_specs=placed, out_specs=P("row", "col"), check_vma=False
    )
```

```python
import functools
import math

import jax
import jax.numpy as jnp
from jax import lax
from jax.experimental import pallas as pl
from jax.experimental.pallas import tpu as pltpu
from jax.sharding import PartitionSpec as P

STEPS = 50
C = 320
ROWS = 8
COLS = 16
PAIR = 2 * C
TALL = 64
PAIRS = 32
CHUNK = 16
CELLS = CHUNK * 32
SHIFTS = (-4, -1, 0, 1, 4)
KEYS = 6144
PITCH = 20
MESH = pl.DeviceIdType.MESH
VMEM_LIMIT = 60 * 1024 * 1024


def silu(x):
    half = 0.5 * x
    return half + half * jnp.tanh(half)


def factors(timestep):
    angle = jnp.full((8, 128), timestep[0].astype(jnp.float32) * (math.pi / STEPS), jnp.float32)
    mix = (1.0 + jnp.cos(angle)) * 0.5
    skip = mix * mix * mix
    gain = (1.0 - skip) * mix
    return tuple(v[0:1, 0:1] for v in ((1.0 - mix) / mix, skip / gain, 1.0 - skip, gain))


def tap_pieces(parity):
    out = []
    for s in (1, 2, 3):
        if parity == 0:
            out += [(s, -1, 2, 3), (s, 0, 0, 5)]
        else:
            out += [(s, 0, 0, 5), (s, 1, 0, 3)]
    first = 0 if parity == 0 else 2
    for s in (0, 2, 4):
        for off in (-2, 0, 2):
            if s == 2 and off == 0:
                continue
            out.append((s, off, first, 3))
    return out


def whole_kernel(
    timestep, fine, coarse_row, coarse_first, coarse_second, local_weight, dilated_weight, out,
    raw, shifted, taps_raw, taps, packed, edges, corner_out, corners, row_in, window_row, patch_in, blocks, acc, staged,
    lifted, grid, cells1, cells2, cells3, keys, turned,
    in_sem, w_sem, out_sem, send_sem, recv_sem, patch_send, patch_recv, pass_send, pass_recv,
):
    f32, bf = jnp.float32, jnp.bfloat16
    r = lax.axis_index("row")
    c = lax.axis_index("col")
    above = r > 0
    below = r < ROWS - 1

    def present(dr, dc):
        ok = None
        for cond, need in ((above, dr < 0), (below, dr > 0), (c > 0, dc < 0), (c < COLS - 1, dc > 0)):
            if need:
                ok = cond if ok is None else jnp.logical_and(ok, cond)
        return ok

    row_load = pltpu.make_async_copy(coarse_row, row_in, in_sem.at[PAIRS])
    row_load.start()
    loads = []
    for p in range(PAIRS):
        cp = pltpu.make_async_copy(fine.at[:, pl.ds(PAIR * p, PAIR)], raw.at[p + 2], in_sem.at[p])
        cp.start()
        loads.append(cp)

    barrier = pltpu.get_barrier_semaphore()

    def greet(dev):
        pl.semaphore_signal(barrier, inc=1, device_id=dev, device_id_type=MESH)

    def greet_row(step, _):
        greet((r, lax.rem(c + step, COLS)))
        return 0

    lax.fori_loop(1, COLS, greet_row, 0)
    diagonal = ((-1, -1), (-1, 0), (-1, 1), (1, -1), (1, 0), (1, 1))
    expected = jnp.int32(COLS - 1)
    for step in diagonal:
        @pl.when(present(*step))
        def _(step=step):
            greet((r + step[0], c + step[1]))
        expected = expected + jnp.where(present(*step), 1, 0)
    side_zero = jnp.zeros((2, TALL, PAIR), bf)

    @pl.when(c == 0)
    def _():
        raw[0:2] = side_zero
        corners[0] = jnp.zeros((8, PAIR), bf)
        corners[2] = jnp.zeros((8, PAIR), bf)

    @pl.when(c == COLS - 1)
    def _():
        raw[34:36] = side_zero
        corners[1] = jnp.zeros((8, PAIR), bf)
        corners[3] = jnp.zeros((8, PAIR), bf)

    @pl.when(jnp.logical_not(above))
    def _():
        edges[0] = jnp.zeros((8, 16, PAIR), bf)
        corners[0] = jnp.zeros((8, PAIR), bf)
        corners[1] = jnp.zeros((8, PAIR), bf)
        patch_in[0:3] = jnp.zeros((3, 3, 8, 384), bf)

    @pl.when(jnp.logical_not(below))
    def _():
        edges[1] = jnp.zeros((8, 16, PAIR), bf)
        corners[2] = jnp.zeros((8, PAIR), bf)
        corners[3] = jnp.zeros((8, PAIR), bf)
        patch_in[19:22] = jnp.zeros((3, 3, 8, 384), bf)

    for cp in loads:
        cp.wait()
    w_loads = []
    for k, ref in enumerate((dilated_weight, local_weight, coarse_first, coarse_second)):
        cp = pltpu.make_async_copy(ref, taps_raw.at[k], w_sem.at[k])
        cp.start()
        w_loads.append(cp)
    for slot, base, first in ((0, 0, 0), (1, 48, 12)):
        tops = {}
        for p in range(PAIRS):
            tops[p] = raw[2 + p, base : base + 16, :].astype(f32)[first : first + 4]
        for q in range(8):
            packed[slot, q] = jnp.concatenate([tops[8 * g + q] for g in range(4)], axis=0).astype(bf)
        for k, p in ((0, 30), (1, 0)):
            spot = k if slot == 1 else 2 + k
            corner_out[spot] = jnp.concatenate([tops[p], tops[p + 1]], axis=0).astype(bf)
    pl.semaphore_wait(barrier, expected)

    last = pl.ds(32, 2)
    head = pl.ds(2, 2)
    sides = (
        ((0, 1), raw.at[last], raw.at[pl.ds(0, 2)]),
        ((0, -1), raw.at[head], raw.at[pl.ds(34, 2)]),
        ((1, 0), packed.at[1], edges.at[0]),
        ((-1, 0), packed.at[0], edges.at[1]),
        ((1, 1), corner_out.at[0], corners.at[0]),
        ((1, -1), corner_out.at[1], corners.at[1]),
        ((-1, 1), corner_out.at[2], corners.at[2]),
        ((-1, -1), corner_out.at[3], corners.at[3]),
    )

    def side_copy(k):
        step, src, dst = sides[k]
        return pltpu.make_async_remote_copy(
            src_ref=src, dst_ref=dst, send_sem=send_sem.at[k], recv_sem=recv_sem.at[k],
            device_id=(r + step[0], c + step[1]), device_id_type=MESH)

    for k in range(8):
        @pl.when(present(*sides[k][0]))
        def _(k=k):
            side_copy(k).start()

    def window(target):
        return window_row.at[pl.ds(2 * target, 3)]

    def patch_copy(dev_c):
        return pltpu.make_async_remote_copy(
            src_ref=window(dev_c), dst_ref=patch_in.at[c + 3], send_sem=patch_send.at[dev_c],
            recv_sem=patch_recv.at[c + 3], device_id=(r, dev_c), device_id_type=MESH)

    row_load.wait()
    turned_row = jnp.concatenate([row_in[...].astype(f32), jnp.zeros((64, 256), f32)], axis=0)
    wide_row = jnp.concatenate(
        [jnp.zeros((4, 384), f32), jnp.transpose(turned_row), jnp.zeros((12, 384), f32)], axis=0)
    window_row[...] = wide_row.reshape(34, 8, 384).astype(bf)
    own = pltpu.make_async_copy(window(c), patch_in.at[c + 3], patch_recv.at[c + 3])
    own.start()

    def send_row(step, _):
        patch_copy(lax.rem(c + step, COLS)).start()
        return 0

    lax.fori_loop(1, COLS, send_row, 0)
    ratio, lift, keep, gain = factors(timestep)

    for cp in w_loads:
        cp.wait()
    gap = jnp.zeros((C, 64), bf)
    dilated = lambda a, b: taps_raw[0, 3 * a + b]
    local = lambda a, b: (ratio * taps_raw[1, 3 * a + b].astype(f32)).astype(bf)
    def fill_taps(par):
        at = 0
        for a in range(3):
            row = []
            for b in range(3):
                if a == 1 and b == 1:
                    row.append((dilated(1, 1).astype(f32) + ratio * taps_raw[1, 4].astype(f32)).astype(bf))
                else:
                    row.append(local(a, b))
            row = [gap] + row if par == 0 else row + [gap]
            taps[par, :, at : at + 1024] = jnp.concatenate(row, axis=1)
            at += 1024
        for a in range(3):
            for b in range(3):
                if a == 1 and b == 1:
                    continue
                w = dilated(a, b)
                taps[par, :, at : at + 384] = jnp.concatenate([w, gap] if par == 0 else [gap, w], axis=1)
                at += 384

    fill_taps(0)

    contract = (((1,), (1,)), ((), ()))

    lane = lax.broadcasted_iota(jnp.int32, (TALL, 256), 1)
    group = jnp.zeros((TALL, 256), jnp.int32)
    for t in range(1, 13):
        group = group + (lane >= PITCH * t).astype(jnp.int32)
    lane_row = (lane - PITCH * group + (16 * r - 1)).astype(f32)
    lane_col = (group[0:8] + (16 * c - 1)).astype(f32)
    fine_row = (lax.broadcasted_iota(jnp.int32, (TALL, 256), 0) + 64 * r).astype(f32)
    where_row = jnp.clip((fine_row + 0.5) * 0.25 - 0.5, 0.0, 127.0)
    row_share = jnp.maximum(1.0 - jnp.abs(where_row - lane_row), 0.0)
    base_col = (jnp.zeros((8, 256), jnp.int32) + 64 * c).astype(f32)
    inner = row_share[16:48].reshape(4, 8, 256)
    outer = jnp.concatenate([row_share[0:16], row_share[48:64]], axis=0).reshape(4, 8, 256)

    def shares(h, par, rim):
        out = []
        for pp in range(CHUNK):
            spot = jnp.clip((base_col + (32 * h + 2 * pp + par + 0.5)) * 0.25 - 0.5, 0.0, 255.0)
            col_share = jnp.maximum(1.0 - jnp.abs(spot - (lane_col + 8 * h)), 0.0)
            part = ((outer if rim else inner) * col_share[None]).reshape(32, 256)
            out.append(jnp.concatenate([part, part], axis=1).astype(bf))
        return jnp.concatenate(out, axis=0)

    def keys_of(h, par, rim):
        pieces = []
        for s, off, tile, n in tap_pieces(par):
            cells = pl.ds(2 + CHUNK * h + off, CHUNK)
            lanes = slice(128 * tile, 128 * (tile + n))
            if rim:
                part = jnp.concatenate([shifted[s, cells, 0:16, lanes], shifted[s, cells, 48:64, lanes]], axis=1)
            else:
                part = shifted[s, cells, 16:48, lanes]
            pieces.append(part.reshape(CELLS, 128 * n))
        return pieces

    def arrived(k):
        step = sides[k][0]

        @pl.when(present(-step[0], -step[1]))
        def _():
            side_copy(k).wait_recv()

    def first_part(p, _):
        values = silu(raw[p].astype(f32))
        lifted[p, 8:72, :] = values
        shifted[2, p] = values.astype(bf)
        for k in (0, 1, 3, 4):
            s = SHIFTS[k]
            shifted[k, p, 16:48, :] = lifted[p, 24 + s : 56 + s, :].astype(bf)
        return 0

    def second_part(p):
        for k in (0, 1, 3, 4):
            s = SHIFTS[k]
            shifted[k, p, 0:16, :] = lifted[p, 8 + s : 24 + s, :].astype(bf)
            shifted[k, p, 48:64, :] = lifted[p, 56 + s : 72 + s, :].astype(bf)

    def convolve(h, par, rim, lifts=False):
        pieces = keys_of(h, par, rim)
        lhs = taps[par]
        if lifts:
            pieces = pieces + [shares(h, par, rim)]
            lhs = jnp.concatenate([lhs, blocks[h]], axis=1)
        acc[2 * h + rim, C * par : C * par + C, :] = lax.dot_general(
            lhs, jnp.concatenate(pieces, axis=1), contract, preferred_element_type=f32)

    def raise_by(h, par, rim):
        acc[2 * h + rim, C * par : C * par + C, :] += lax.dot_general(
            blocks[h], shares(h, par, rim), contract, preferred_element_type=f32)

    lax.fori_loop(2, 20, first_part, 0)

    passes = (
        (below, 1, patch_in.at[pl.ds(16, 3)], patch_in.at[pl.ds(0, 3)]),
        (above, -1, patch_in.at[pl.ds(3, 3)], patch_in.at[pl.ds(19, 3)]),
    )

    def pass_copy(k):
        cond, step, src, dst = passes[k]
        return pltpu.make_async_remote_copy(
            src_ref=src, dst_ref=dst, send_sem=pass_send.at[k], recv_sem=pass_recv.at[k],
            device_id=(r + step, c), device_id_type=MESH)

    arrived(0)
    arrived(1)
    first_part(0, 0)
    first_part(1, 0)
    convolve(0, 0, False)
    fill_taps(1)
    for p in range(20, 28):
        first_part(p, 0)
    convolve(0, 1, False)
    for p in range(28, 36):
        first_part(p, 0)
    convolve(1, 0, False)
    def got(k):
        pltpu.make_async_copy(window_row.at[pl.ds(0, 3)], patch_in.at[k], patch_recv.at[k]).wait()

    for k in (3, 4, 5, 16, 17, 18):
        got(k)
    for k in range(2):
        @pl.when(passes[k][0])
        def _(k=k):
            pass_copy(k).start()

    convolve(1, 1, False)
    for k in range(2, 8):
        arrived(k)
    for slot, base in ((0, 4), (1, 72)):
        for q in range(8):
            block = silu(edges[slot, q].astype(f32))
            for g in range(4):
                lifted[2 + 8 * g + q, base : base + 4, :] = block[4 * g : 4 * g + 4]
        for k, first in ((0, 0), (1, 34)):
            block = silu(corners[2 * slot + k].astype(f32))
            for p in range(2):
                lifted[first + p, base : base + 4, :] = block[4 * p : 4 * p + 4]
    for p in range(20):
        second_part(p)
    convolve(0, 0, True)
    for p in range(20, 36):
        second_part(p)

    for k in range(6, 16):
        got(k)
    for k, cond in ((0, above), (1, below)):
        @pl.when(cond)
        def _(k=k):
            pass_copy(k).wait_recv()

    values = patch_in[...].astype(f32).reshape(22 * 24, 384)
    for t in range(3):
        grid[t] = silu(values[:, 128 * t : 128 * t + 128])
    cells1[520:568, :] = jnp.zeros((48, 384), f32)
    cells2[400:432, :] = jnp.zeros((32, 384), f32)
    cells3[360:384, :] = jnp.zeros((24, 384), f32)
    for t in range(3):
        lanes = slice(128 * t, 128 * t + 128)
        for m in range(22):
            cells1[24 * m : 24 * m + 24, lanes] = jnp.concatenate(
                [grid[t, pl.ds(m + 1, 22, stride=24), :], jnp.zeros((2, 128), f32)], axis=0)
    for t in range(3):
        grid[t] = values[:, 128 * t : 128 * t + 128]
    for t in range(3):
        lanes = slice(128 * t, 128 * t + 128)
        for m in range(18):
            cells3[PITCH * m : PITCH * m + PITCH, lanes] = grid[t, pl.ds(48 + m + 3, PITCH, stride=24), :]
    for a in range(3):
        for b in range(3):
            k = 3 * a + b
            first = 24 * b + a
            keys[:, 384 * k : 384 * k + 384] = cells1[first : first + 512, :].astype(bf)
    convolve(0, 1, True)
    widen = lambda w: jnp.concatenate([w, gap], axis=1)
    first_taps = jnp.concatenate([widen(taps_raw[2, k]) for k in range(9)], axis=1)
    hidden = lax.dot_general(first_taps, keys[:, 0:3456], contract, preferred_element_type=f32)
    hidden = jnp.concatenate([silu(hidden), jnp.zeros((64, 512), f32)], axis=0)
    turned[...] = jnp.transpose(hidden)
    field_row = lax.broadcasted_iota(jnp.int32, (PITCH, 384), 0) + (16 * r - 2)
    row_ok = jnp.logical_and(field_row >= 0, field_row < 128)
    for m in range(20):
        col = 16 * c - 2 + m
        ok = jnp.logical_and(row_ok, jnp.logical_and(col >= 0, col < 256))
        cells2[PITCH * m : PITCH * m + PITCH, :] = jnp.where(ok, turned[24 * m : 24 * m + PITCH, :], 0.0)
    for a in range(3):
        for b in range(3):
            k = 3 * a + b
            first = PITCH * b + a
            keys[0:384, 384 * k : 384 * k + 384] = cells2[first : first + 384, :].astype(bf)
    keys[0:384, 3456:3840] = cells3[...].astype(bf)
    eye = lax.broadcasted_iota(jnp.int32, (C, 384), 0) == lax.broadcasted_iota(jnp.int32, (C, 384), 1)
    second_taps = jnp.concatenate([widen(taps_raw[3, k]) for k in range(9)] + [eye.astype(f32).astype(bf)], axis=1)
    coarse = lift * lax.dot_general(second_taps, keys[0:384, :], contract, preferred_element_type=f32)
    for h in range(2):
        part = coarse if h == 0 else pltpu.roll(coarse, 384 - 160, axis=1)
        part = part[:, 0:256]
        high = part.astype(bf)
        blocks[h, :, 0:256] = high
        blocks[h, :, 256:512] = (part - high.astype(f32)).astype(bf)
    writes = {}

    def blend(h, rim, source, slot):
        for old in writes.pop(slot, ()):
            old.wait()
        for u in range(CHUNK // 4):
            block = jnp.transpose(acc[source, :, 128 * u : 128 * u + 128])
            for v in range(4):
                pp = 4 * u + v
                cells = raw[2 + CHUNK * h + pp]
                if rim:
                    cells = jnp.concatenate([cells[0:16], cells[48:64]], axis=0)
                else:
                    cells = cells[16:48]
                staged[slot, :, PAIR * pp : PAIR * (pp + 1)] = (
                    keep * cells.astype(f32) + gain * block[32 * v : 32 * v + 32])
        lanes = pl.ds(PAIR * CHUNK * h, PAIR * CHUNK)
        if rim:
            parts = [(pl.ds(0, 16), pl.ds(0, 16)), (pl.ds(16, 16), pl.ds(48, 16))]
        else:
            parts = [(pl.ds(0, 32), pl.ds(16, 32))]
        writes[slot] = []
        for k, (here, there) in enumerate(parts):
            cp = pltpu.make_async_copy(staged.at[slot, here], out.at[there, lanes], out_sem.at[2 * slot + k])
            cp.start()
            writes[slot].append(cp)

    def raised(h, rim):
        for par in range(2):
            raise_by(h, par, rim)

    raised(0, False)
    raised(0, True)
    blend(0, False, 0, 0)
    convolve(1, 0, True, True)
    blend(0, True, 1, 1)
    raised(1, False)
    blend(1, False, 2, 0)
    convolve(1, 1, True, True)
    blend(1, True, 3, 1)
    for group_of in writes.values():
        for cp in group_of:
            cp.wait()

    for k in range(8):
        @pl.when(present(*sides[k][0]))
        def _(k=k):
            side_copy(k).wait_send()

    def sent_row(step, _):
        patch_copy(lax.rem(c + step, COLS)).wait_send()
        return 0

    lax.fori_loop(1, COLS, sent_row, 0)
    for k in range(2):
        @pl.when(passes[k][0])
        def _(k=k):
            pass_copy(k).wait_send()


def whole(*arrays):
    f32, bf = jnp.float32, jnp.bfloat16
    any_spec = pl.BlockSpec(memory_space=pl.ANY)
    return pl.pallas_call(
        whole_kernel,
        out_shape=jax.ShapeDtypeStruct((64, 20480), f32),
        in_specs=[pl.BlockSpec(memory_space=pltpu.SMEM)] + [any_spec] * 6,
        out_specs=any_spec,
        scratch_shapes=[
            pltpu.VMEM((36, 64, 640), bf),
            pltpu.VMEM((5, 36, 64, 640), bf),
            pltpu.VMEM((4, 9, C, C), bf),
            pltpu.VMEM((2, C, KEYS), bf),
            pltpu.VMEM((2, 8, 16, 640), bf),
            pltpu.VMEM((2, 8, 16, 640), bf),
            pltpu.VMEM((4, 8, 640), bf),
            pltpu.VMEM((4, 8, 640), bf),
            pltpu.VMEM((C, 256), bf),
            pltpu.VMEM((34, 8, 384), bf),
            pltpu.VMEM((22, 3, 8, 384), bf),
            pltpu.VMEM((2, C, 512), bf),
            pltpu.VMEM((4, PAIR, CELLS), f32),
            pltpu.VMEM((2, 32, PAIR * CHUNK), f32),
            pltpu.VMEM((36, 80, 640), f32),
            pltpu.VMEM((3, 528, 128), f32),
            pltpu.VMEM((568, 384), f32),
            pltpu.VMEM((432, 384), f32),
            pltpu.VMEM((384, 384), f32),
            pltpu.VMEM((512, 3840), bf),
            pltpu.VMEM((512, 384), f32),
            pltpu.SemaphoreType.DMA((PAIRS + 1,)),
            pltpu.SemaphoreType.DMA((4,)),
            pltpu.SemaphoreType.DMA((4,)),
            pltpu.SemaphoreType.DMA((8,)),
            pltpu.SemaphoreType.DMA((8,)),
            pltpu.SemaphoreType.DMA((COLS,)),
            pltpu.SemaphoreType.DMA((22,)),
            pltpu.SemaphoreType.DMA((2,)),
            pltpu.SemaphoreType.DMA((2,)),
        ],
        compiler_params=pltpu.CompilerParams(collective_id=0, has_side_effects=True, vmem_limit_bytes=VMEM_LIMIT),
        name="whole",
    )(*arrays)


def store_kernel(held, out, block, in_sem, out_sem):
    lanes = [pl.ds(1280 * k, 1280) for k in range(16)]
    reads = [pltpu.make_async_copy(held.at[:, lanes[k]], block.at[k], in_sem.at[k]) for k in range(16)]
    writes = [pltpu.make_async_copy(block.at[k], out.at[:, lanes[k]], out_sem.at[k]) for k in range(16)]
    for cp in reads:
        cp.start()
    for k in range(16):
        reads[k].wait()
        writes[k].start()
    for cp in writes:
        cp.wait()


def store(held):
    any_spec = pl.BlockSpec(memory_space=pl.ANY)
    return pl.pallas_call(
        store_kernel,
        out_shape=jax.ShapeDtypeStruct((64, 20480), jnp.float32),
        in_specs=[any_spec],
        out_specs=any_spec,
        scratch_shapes=[
            pltpu.VMEM((16, 64, 1280), jnp.float32),
            pltpu.SemaphoreType.DMA((16,)),
            pltpu.SemaphoreType.DMA((16,)),
        ],
        compiler_params=pltpu.CompilerParams(vmem_limit_bytes=VMEM_LIMIT),
        name="store",
    )(held)


def on_device(coarse_latent, fine_latent, timestep, coarse_first, coarse_second, local_weight, dilated_weight):
    flat = lambda w: w.reshape(9, C, C)
    held = whole(
        timestep, fine_latent, coarse_latent.reshape(C, 256),
        flat(coarse_first), flat(coarse_second), flat(local_weight), flat(dilated_weight))
    return store(held)


def solution(mesh):
    placed = (P(None, ("row", "col"), None), P("row", "col"), P(), P(), P(), P(), P())
    return jax.shard_map(
        on_device, mesh=mesh, in_specs=placed, out_specs=P("row", "col"), check_vma=False
    )
```
